256 devices in a mesh: mem: 16 (over z, core), gx: 4 (over x), gy: 4 (over y).
Axes of the slice: x: 4, y: 4, z: 8, core: 2. Of those that a mesh axis runs over, the one named last changes fastest.
Arguments:
- state: bfloat16 [2048, 128, 4, 256], P(('gx', 'gy'), 'mem'), may hold values from -6 to 6
- obs_ens: float32 [128, 4, 4, 8192], P('mem', 'gx', 'gy'), may hold values from -6 to 6
- obs_values: float32 [2, 4, 4, 8192], P(None, 'gx', 'gy'), may hold values from -4 to 4, as said below
- obs_index: int32 [2048, 128], P(('gx', 'gy')), may hold values from 0 to 67583, as said below
- patch_count: int32 [2048], P(('gx', 'gy')), may hold values from 32 to 128
- slot_weight: float32 [2048, 128], P(('gx', 'gy')), may hold values from 0.05 to 1
Outputs:
- analysis: bfloat16 [2048, 128, 4, 256], P(('gx', 'gy'), 'mem')
The draws below stay inside these ranges and needn't reach their ends.
Inputs may be any that keep to these rules, and one draw needn't show every extreme that they name: `obs_index`: every tile's list holds 8192 observations. A slot names another tile only at positions below 2048, and never a tile outside the grid. Slots at or beyond a patch's count hold valid codes too. `obs_values`: component 1 is positive.
All inputs are finite; a program needn't handle non-finite values.
Results may differ from the reference program's by a relative error of at most 0.006.
Values may be sent and summed in bfloat16 or wider, within the bound.
A program may use at most 128 MiB of HBM per device.

```python
import jax
import jax.numpy as jnp
from jax import lax

MEMBERS = 128
LEV = 4
PATCH_COLS = 256
SLOTS = 128
NS = 6
PATCH_T = 128
OBS_T = 8192
RIM_T = 2048
TILES_X = 4
TILES_Y = 4
NPATCH = 2048


def draw_obs_values(key, part):
    key = jax.random.fold_in(key, 13)
    first_key, second_key = jax.random.split(key)
    shape = (TILES_X, TILES_Y, OBS_T)
    observed = jnp.clip(jax.random.normal(first_key, shape, jnp.float32), -4.0, 4.0)
    obs_rate = jnp.exp(jax.random.uniform(second_key, shape, jnp.float32, jnp.log(0.1), jnp.log(2.0)))
    return jnp.stack([observed, obs_rate])


def draw_obs_index(key, part):
    key = jax.random.fold_in(key, 11)
    keys = jax.random.split(key, 5)
    shape = (NPATCH, SLOTS)
    patch_ids = jnp.arange(NPATCH, dtype=jnp.int32)[:, None]
    tile_ids = patch_ids // PATCH_T
    tile_row = tile_ids // TILES_Y
    tile_col = tile_ids % TILES_Y
    nearby = jax.random.randint(keys[0], shape, 0, 4) == 0
    step_x = jax.random.randint(keys[1], shape, -1, 2)
    step_y = jax.random.randint(keys[2], shape, -1, 2)
    step_x = jnp.where(nearby & (tile_row + step_x >= 0) & (tile_row + step_x < TILES_X), step_x, 0)
    step_y = jnp.where(nearby & (tile_col + step_y >= 0) & (tile_col + step_y < TILES_Y), step_y, 0)
    codes = (step_x + 1) * 3 + (step_y + 1)
    own_pos = jax.random.randint(keys[3], shape, 0, OBS_T)
    rim_pos = jax.random.randint(keys[4], shape, 0, RIM_T)
    offsets = jnp.where(codes == 4, own_pos, rim_pos)
    indices = (codes * OBS_T + offsets).astype(jnp.int32)
    indices = indices.at[0, 0].set(8 * OBS_T + RIM_T - 1)
    indices = indices.at[0, 1].set(5 * OBS_T - 1)
    indices = indices.at[NPATCH - 1, 0].set(0)
    return indices


def draw_patch_count(key, part):
    key = jax.random.fold_in(key, 12)
    first_key, second_key = jax.random.split(key)
    filled = jax.random.randint(first_key, (NPATCH,), 0, 10) < 3
    partial_count = jax.random.randint(second_key, (NPATCH,), SLOTS // 4, SLOTS + 1)
    counts = jnp.where(filled, SLOTS, partial_count).astype(jnp.int32)
    counts = counts.at[0].set(SLOTS)
    counts = counts.at[1].set(SLOTS // 4)
    return counts


def level_of(rng, dims, shards, low, top_value):
    def one(axis_at, parts):
        steps = jax.random.uniform(jax.random.fold_in(jax.random.fold_in(rng, 6), axis_at), (parts,), jnp.float32, low / len(shards), top_value / len(shards))
        return jnp.repeat(jnp.exp(steps), dims[axis_at] // parts).reshape((-1,) + (1,) * (len(dims) - axis_at - 1))

    factor_of = one(*shards[0])
    for cut in shards[1:]:
        factor_of = factor_of * one(*cut)
    return factor_of


def scatter_about(key, dims, width, bound, cuts=(), held_as=jnp.bfloat16):
    drawn = jax.random.normal(key, dims, jnp.float32) * width
    if len(cuts) > 0:
        drawn = level_of(key, dims, cuts, -0.22, 0.18) * drawn
    return jnp.clip(drawn, min=-bound, max=bound).astype(held_as)


def setup_inputs(seed: int = 0) -> dict:
    streams_of = jax.random.split(jax.random.key(seed), 7)
    state = scatter_about(streams_of[0], (NPATCH, MEMBERS, LEV, PATCH_COLS), 1.0, 6.0, ((0, 16), (1, 16)))
    obs_ens = scatter_about(streams_of[1], (MEMBERS, TILES_X, TILES_Y, OBS_T), 1.0, 6.0, ((0, 16), (1, 4), (2, 4)), jnp.float32)
    obs_values = draw_obs_values(jax.random.fold_in(streams_of[6], 71), 0)
    obs_index = draw_obs_index(jax.random.fold_in(streams_of[6], 71), 0)
    patch_count = draw_patch_count(jax.random.fold_in(streams_of[6], 71), 0)
    slot_weight = jnp.clip(0.05 + 0.95 * jax.random.uniform(streams_of[5], (NPATCH, SLOTS), jnp.float32) ** level_of(streams_of[5], (NPATCH, SLOTS), ((0, 16),), -0.2, 0.2), 0.05, 1.0)
    return dict(state=state, obs_ens=obs_ens, obs_values=obs_values, obs_index=obs_index, patch_count=patch_count, slot_weight=slot_weight)


HIGHEST = lax.Precision.HIGHEST

def patch_weights(chosen, observed, obs_rate, ens_size):
    mean_obs = lax.optimization_barrier(jnp.mean(chosen, axis=0))
    spread = chosen - mean_obs
    misfit = observed - mean_obs
    gram_mat = jnp.einsum('jps,kps->pjk', spread * obs_rate, spread, precision=HIGHEST)
    identity = jnp.eye(ens_size, dtype=jnp.float32)
    system = gram_mat + (ens_size - 1.0) * identity
    frob_norm = jnp.sqrt(lax.optimization_barrier(jnp.sum(system * system, axis=(1, 2))))[:, None, None]
    root_est = system / frob_norm
    inverse = jnp.broadcast_to(identity, system.shape)
    for sweep_id in range(NS):
        factor = 1.5 * identity - 0.5 * jnp.einsum('pij,pjk->pik', inverse, root_est, precision=HIGHEST)
        root_est = jnp.einsum('pij,pjk->pik', root_est, factor, precision=HIGHEST)
        inverse = jnp.einsum('pij,pjk->pik', factor, inverse, precision=HIGHEST)
    inv_half = inverse / jnp.sqrt(frob_norm)
    covariance = jnp.einsum('pij,pjk->pik', inv_half, inv_half, precision=HIGHEST)
    pulled = jnp.einsum('jps,ps->pj', spread, obs_rate * misfit, precision=HIGHEST)
    mean_shift = jnp.einsum('pjk,pk->pj', covariance, pulled, precision=HIGHEST)
    transform = jnp.sqrt(ens_size - 1.0) * inv_half + mean_shift[:, :, None]
    return transform.astype(jnp.bfloat16)

def apply_weights(state_block, transform):
    widened = state_block.astype(jnp.float32)
    mean_state = lax.optimization_barrier(jnp.mean(widened, axis=1))
    perturb = (widened - mean_state[:, None]).astype(jnp.bfloat16)
    mixed_sum = jnp.einsum('pjlc,pjk->pklc', perturb.astype(jnp.float32), transform.astype(jnp.float32), precision=HIGHEST)
    return (mixed_sum + mean_state[:, None]).astype(jnp.bfloat16)

def reference(state, obs_ens, obs_values, obs_index, patch_count, slot_weight):
    ens_size = state.shape[1]
    ens_pad = jnp.pad(obs_ens, ((0, 0), (1, 1), (1, 1), (0, 0)))
    val_pad = jnp.pad(obs_values, ((0, 0), (1, 1), (1, 1), (0, 0)))
    slot_ids = jnp.arange(SLOTS, dtype=jnp.int32)

    def one_tile(tile_id):
        tile_row = (tile_id // TILES_Y).astype(jnp.int32)
        tile_col = (tile_id % TILES_Y).astype(jnp.int32)
        anchor = jnp.zeros((), jnp.int32)
        obs_pool = lax.dynamic_slice(ens_pad, (anchor, tile_row, tile_col, anchor), (ens_size, 3, 3, OBS_T)).reshape(ens_size, 9 * OBS_T)
        val_pool = lax.dynamic_slice(val_pad, (anchor, tile_row, tile_col, anchor), (2, 3, 3, OBS_T)).reshape(2, 9 * OBS_T)
        first_patch = (tile_id * PATCH_T).astype(jnp.int32)
        indices = lax.dynamic_slice_in_dim(obs_index, first_patch, PATCH_T, 0).reshape(-1)
        chosen = jnp.take(obs_pool, indices, axis=1).reshape(ens_size, PATCH_T, SLOTS)
        picked = jnp.take(val_pool, indices, axis=1).reshape(2, PATCH_T, SLOTS)
        counts = lax.dynamic_slice_in_dim(patch_count, first_patch, PATCH_T, 0)
        weights = lax.dynamic_slice_in_dim(slot_weight, first_patch, PATCH_T, 0)
        obs_rate = picked[1] * weights * (slot_ids[None, :] < counts[:, None]).astype(jnp.float32)
        transform = patch_weights(chosen, picked[0], obs_rate, ens_size)
        state_block = lax.dynamic_slice_in_dim(state, first_patch, PATCH_T, 0)
        return apply_weights(state_block, transform)
    results = lax.map(one_tile, jnp.arange(TILES_X * TILES_Y, dtype=jnp.int32))
    return results.reshape(state.shape)
```

```python
import math

import jax
import jax.numpy as jnp
from jax import lax
from jax.experimental import pallas as pl
from jax.experimental.pallas import tpu as pltpu
from jax.sharding import PartitionSpec as P

NS = 6
MESH = pl.DeviceIdType.MESH
F32 = jnp.float32
BF16 = jnp.bfloat16

GROUP = 16
SHARE = 8
SLOTS = 128
ENS = GROUP * SHARE
PATCHES = GROUP * SHARE
OBS = 8192
RIM = 2048
CHUNK = 256
OWN_CHUNKS = OBS // CHUNK
RIM_CHUNKS = RIM // CHUNK
CHUNKS = OWN_CHUNKS + 8 * RIM_CHUNKS
MSG = SHARE * SHARE + 2 * SHARE
EARLY = 3

SIDES = [(dx, dy) for dx in (-1, 0, 1) for dy in (-1, 0, 1) if (dx, dy) != (0, 0)]


def split(a):
    high = a.astype(BF16)
    return high, (a - high.astype(F32)).astype(BF16)


def mm(a, b):
    a_high, a_low = split(a)
    b_high, b_low = split(b)
    row = jnp.concatenate([b_high, b_low], axis=1)
    out = jnp.dot(
        jnp.concatenate([a_high, a_low], axis=1),
        jnp.concatenate([row, row], axis=0),
        preferred_element_type=F32,
    )
    width = b.shape[1]
    return out[:, :width] + out[:, width:]


def mm_t(a, b):
    a_high, a_low = split(a)
    b_high, b_low = split(b)
    out = lax.dot_general(
        jnp.concatenate([a_high, a_low], axis=1),
        jnp.concatenate(
            [
                jnp.concatenate([b_high, b_high], axis=1),
                jnp.concatenate([b_low, b_low], axis=1),
            ],
            axis=0,
        ),
        (((1,), (1,)), ((), ())),
        preferred_element_type=F32,
    )
    width = b.shape[0]
    return out[:, :width] + out[:, width:]


def kernel(
    state, ens, vals, index, counts, weights, out,
    ens_raw, vals_raw, ens_rim, vals_rim, index_v, weights_v, counts_v,
    pool, mean_f, mean_pool, val_pool, obs_own, rate_own,
    msg_out, msg_in, state_in, root, pulled_s, frob_s, trans, wide, mixed, back,
    local_sem, rim_send, rim_recv, val_send, val_recv,
    msg_send, msg_recv, msg_own, state_send, state_recv, state_own,
    back_send, back_recv, back_own,
):
    me = lax.axis_index("mem")
    tile_x = lax.axis_index("gx")
    tile_y = lax.axis_index("gy")

    loads = [
        pltpu.make_async_copy(ens, ens_raw, local_sem.at[0]),
        pltpu.make_async_copy(vals, vals_raw, local_sem.at[1]),
        pltpu.make_async_copy(index, index_v, local_sem.at[2]),
        pltpu.make_async_copy(
            weights.at[pl.ds(pl.multiple_of(me * SHARE, SHARE), SHARE)],
            weights_v, local_sem.at[3],
        ),
        pltpu.make_async_copy(counts, counts_v, local_sem.at[4]),
    ]

    def tile_at(dx, dy):
        return {
            "gx": lax.rem(tile_x + dx + 4, 4),
            "gy": lax.rem(tile_y + dy + 4, 4),
        }

    barrier = pltpu.get_barrier_semaphore()
    for dx, dy in SIDES:
        pl.semaphore_signal(barrier, inc=1, device_id=tile_at(dx, dy), device_id_type=MESH)
    for step in range(1, GROUP):
        pl.semaphore_signal(
            barrier, inc=1, device_id={"mem": lax.rem(me + step, GROUP)}, device_id_type=MESH
        )
    for load in loads:
        load.start()

    def own_state(patch):
        return pltpu.make_async_copy(
            state.at[me * SHARE + patch], state_in.at[patch, me], state_own.at[patch]
        )

    def send_state(patch):
        def one(step, carry):
            to = lax.rem(me + 5 * step, GROUP)
            pltpu.make_async_remote_copy(
                src_ref=state.at[to * SHARE + patch],
                dst_ref=state_in.at[patch, me],
                send_sem=state_send,
                recv_sem=state_recv.at[patch],
                device_id={"mem": to},
                device_id_type=MESH,
            ).start()
            return carry

        lax.fori_loop(1, GROUP, one, 0)

    for patch in range(SHARE):
        own_state(patch).start()
    pl.semaphore_wait(barrier, len(SIDES) + GROUP - 1)

    loads[0].wait()
    loads[1].wait()
    rims = []
    for side, (dx, dy) in enumerate(SIDES):
        slot = len(SIDES) - 1 - side
        for src, dst, send, recv in (
            (ens_raw, ens_rim, rim_send, rim_recv),
            (vals_raw, vals_rim, val_send, val_recv),
        ):
            copy = pltpu.make_async_remote_copy(
                src_ref=src.at[:, :, :, pl.ds(0, RIM)],
                dst_ref=dst.at[slot],
                send_sem=send.at[slot],
                recv_sem=recv.at[slot],
                device_id=tile_at(dx, dy),
                device_id_type=MESH,
            )
            copy.start()
            rims.append(copy)

    for patch in range(EARLY):
        send_state(patch)

    def fill(chunk_pair, ens_block, vals_block):
        mean = jnp.mean(ens_block, axis=0, keepdims=True)
        dev = ens_block - mean
        rows = pl.ds(pl.multiple_of(chunk_pair * 16, 16), 16)
        pool[rows, :] = jnp.concatenate([dev[:, :CHUNK], dev[:, CHUNK:]], axis=0).astype(BF16)
        mean_f[pl.ds(chunk_pair * 2, 1), :] = mean[:, :CHUNK]
        mean_f[pl.ds(chunk_pair * 2 + 1, 1), :] = mean[:, CHUNK:]
        first = vals_block.astype(BF16).astype(F32)
        rest = vals_block - first
        second = rest.astype(BF16).astype(F32)
        parts = jnp.concatenate([first, second, rest - second, jnp.zeros_like(first)], axis=0)
        val_pool[rows, :] = jnp.concatenate(
            [parts[:, :CHUNK], parts[:, CHUNK:]], axis=0
        ).astype(BF16)

    def fill_own(pair, carry):
        cols = pl.ds(pl.multiple_of(pair * 2 * CHUNK, 2 * CHUNK), 2 * CHUNK)
        fill(
            pair,
            jnp.concatenate([ens_raw[m, 0, :, cols] for m in range(SHARE)], axis=0),
            jnp.concatenate([vals_raw[c, 0, :, cols] for c in range(2)], axis=0),
        )
        return carry

    lax.fori_loop(0, OWN_CHUNKS // 2, fill_own, 0)

    for copy in rims:
        copy.wait()

    def fill_rim(step, carry):
        side = step // (RIM_CHUNKS // 2)
        pair = step % (RIM_CHUNKS // 2)
        cols = pl.ds(pl.multiple_of(pair * 2 * CHUNK, 2 * CHUNK), 2 * CHUNK)
        fill(
            OWN_CHUNKS // 2 + step,
            jnp.concatenate([ens_rim[side, m, 0, :, cols] for m in range(SHARE)], axis=0),
            jnp.concatenate([vals_rim[side, c, 0, :, cols] for c in range(2)], axis=0),
        )
        return carry

    lax.fori_loop(0, 8 * RIM_CHUNKS // 2, fill_rim, 0)
    means = mean_f[...]
    mean_high, mean_low = split(means)
    mean_pool[0:CHUNKS, :] = mean_high
    mean_pool[CHUNKS : 2 * CHUNKS, :] = mean_low

    for load in loads[2:]:
        load.wait()

    sub_iota = lax.broadcasted_iota(jnp.int32, (CHUNK, 2 * SLOTS), 0)
    row_iota = lax.broadcasted_iota(jnp.int32, (8, 2 * SLOTS), 0)

    def pick(table, chunk_of, onehot):
        found = jnp.zeros((8, 2 * SLOTS), F32)
        for block in range(CHUNKS // 16):
            rows = jnp.dot(
                table[block * 128 : (block + 1) * 128, :], onehot, preferred_element_type=F32
            )
            for c in range(16):
                found = jnp.where(chunk_of == block * 16 + c, rows[8 * c : 8 * c + 8], found)
        return found

    def gather(step, carry):
        to = lax.rem(me + 5 * (step + 1), GROUP)
        codes = index_v[pl.ds(pl.multiple_of(to * SHARE, SHARE), SHARE), :]
        tile = codes >> 13
        pos = codes & (OBS - 1)
        side = jnp.where(tile > 4, tile - 1, tile)
        chunk = jnp.where(tile == 4, pos >> 8, OWN_CHUNKS + side * RIM_CHUNKS + (pos >> 8))
        lane = pos & (CHUNK - 1)
        pairs = []
        for pair in range(SHARE // 2):
            two = lambda a: jnp.concatenate(
                [a[2 * pair : 2 * pair + 1], a[2 * pair + 1 : 2 * pair + 2]], axis=1
            )
            onehot = jnp.where(sub_iota == two(lane), 1.0, 0.0).astype(BF16)
            pairs.append((onehot, jnp.broadcast_to(two(chunk), (8, 2 * SLOTS))))
        heads = ([], [])
        for pair, (onehot, chunk_of) in enumerate(pairs):
            dev = pick(pool, chunk_of, onehot)
            msg_out[step, 16 * pair : 16 * pair + 16, :] = jnp.concatenate(
                [dev[:, :SLOTS], dev[:, SLOTS:]], axis=0
            ).astype(BF16)
            rows = jnp.dot(mean_pool[...], onehot, preferred_element_type=F32)
            turned = chunk_of - row_iota
            for part in range(2):
                found = jnp.zeros((8, 2 * SLOTS), F32)
                for k in range(CHUNKS // 8):
                    at = part * CHUNKS + 8 * k
                    found = jnp.where(turned == 8 * k, rows[at : at + 8], found)
                found = jnp.sum(found, axis=0, keepdims=True)
                heads[part].extend([found[:, :SLOTS], found[:, SLOTS:]])
        msg_out[step, SHARE * SHARE : MSG, :] = jnp.concatenate(
            heads[0] + heads[1], axis=0
        ).astype(BF16)

        @pl.when(step < GROUP - 1)
        def _():
            pltpu.make_async_remote_copy(
                src_ref=msg_out.at[step],
                dst_ref=msg_in.at[me],
                send_sem=msg_send,
                recv_sem=msg_recv,
                device_id={"mem": to},
                device_id_type=MESH,
            ).start()

        @pl.when(step == GROUP - 1)
        def _():
            pltpu.make_async_copy(msg_out.at[step], msg_in.at[me], msg_own).start()
            for pair, (onehot, chunk_of) in enumerate(pairs):
                got = pick(val_pool, chunk_of, onehot)
                got = got[0:2] + got[2:4] + got[4:6]
                obs_own[2 * pair : 2 * pair + 1, :] = got[0:1, :SLOTS]
                obs_own[2 * pair + 1 : 2 * pair + 2, :] = got[0:1, SLOTS:]
                rate_own[2 * pair : 2 * pair + 1, :] = got[1:2, :SLOTS]
                rate_own[2 * pair + 1 : 2 * pair + 2, :] = got[1:2, SLOTS:]

        return carry

    lax.fori_loop(0, GROUP, gather, 0)

    for patch in range(EARLY, SHARE):
        send_state(patch)

    msg_all = pltpu.make_async_remote_copy(
        src_ref=msg_out.at[pl.ds(0, GROUP - 1)],
        dst_ref=msg_in.at[pl.ds(0, GROUP - 1)],
        send_sem=msg_send,
        recv_sem=msg_recv,
        device_id={"mem": lax.rem(me + 1, GROUP)},
        device_id_type=MESH,
    )
    msg_all.wait_recv()
    pltpu.make_async_copy(msg_out.at[GROUP - 1], msg_in.at[me], msg_own).wait()

    eye = jnp.where(
        lax.broadcasted_iota(jnp.int32, (ENS, ENS), 0)
        == lax.broadcasted_iota(jnp.int32, (ENS, ENS), 1),
        1.0,
        0.0,
    ).astype(F32)
    lane_iota = lax.broadcasted_iota(jnp.int32, (1, SLOTS), 1)
    counts_row = counts_v[...].reshape(1, PATCHES).astype(F32)
    for p in range(SHARE):
        dev = msg_in[:, SHARE * p : SHARE * p + SHARE, :].astype(F32)
        heads = msg_in[:, SHARE * SHARE : MSG, :].astype(F32)
        head = heads[:, p : p + 1, :] + heads[:, SHARE + p : SHARE + p + 1, :]
        chosen = (dev + head).reshape(ENS, SLOTS)
        mean_obs = jnp.mean(chosen, axis=0, keepdims=True)
        spread = chosen - mean_obs
        count = jnp.sum(
            jnp.where(lane_iota == me * SHARE + p, counts_row, 0.0), axis=1, keepdims=True
        )
        used = lane_iota.astype(F32) < count
        rate = jnp.where(used, rate_own[p : p + 1, :] * weights_v[p : p + 1, :], 0.0)
        misfit = obs_own[p : p + 1, :] - mean_obs
        system = mm_t(spread * rate, spread) + (ENS - 1.0) * eye
        square = jnp.sum(system * system, axis=1, keepdims=True)
        frob = jnp.sqrt(jnp.sum(square, axis=0, keepdims=True))
        pulled_s[p] = mm_t(jnp.broadcast_to(rate * misfit, (8, SLOTS)), spread)
        frob_s[p] = jnp.broadcast_to(frob, (8, SLOTS))
        scaled = system / frob
        change = 0.5 * (eye - scaled)
        root[p, :ENS] = eye + change
        root[p, ENS:] = scaled + mm(scaled, change)

    def sweep(step, carry):
        for p in range(SHARE):
            both = root[p]
            change = 0.5 * (eye - mm(both[:ENS], both[ENS:]))
            root[p] = both + mm(both, change)
        return carry

    lax.fori_loop(1, NS - 1, sweep, 0)
    for p in range(SHARE):
        both = root[p]
        inverse = both[:ENS]
        change = 0.5 * (eye - mm(inverse, both[ENS:]))
        inverse = inverse + mm(inverse, change)
        inv_half = inverse / jnp.sqrt(frob_s[p][0:1, :])
        shift = mm(mm(pulled_s[p], inv_half), inv_half)[0:1]
        trans[p] = (math.sqrt(ENS - 1.0) * inv_half + shift).astype(BF16)

    def analyse(p, carry):
        pltpu.make_async_remote_copy(
            src_ref=state.at[pl.ds(0, GROUP - 1)],
            dst_ref=state_in.at[p, pl.ds(0, GROUP - 1)],
            send_sem=state_send,
            recv_sem=state_recv.at[p],
            device_id={"mem": lax.rem(me + 1, GROUP)},
            device_id_type=MESH,
        ).wait_recv()
        own_state(p).wait()

        def widen(source, carry):
            for m in range(SHARE):
                block = state_in[p, source, m].astype(F32)
                for half in range(2):
                    wide[half, pl.ds(source * SHARE + m, 4, stride=ENS), :] = block[
                        :, 128 * half : 128 * half + 128
                    ]
            return carry

        lax.fori_loop(0, GROUP, widen, 0)
        mix = trans[p]
        for level in range(4):
            for half in range(2):
                rows = slice(ENS * level, ENS * level + ENS)
                block = wide[half, rows, :]
                mean_state = jnp.mean(block, axis=0, keepdims=True)
                perturb = (block - mean_state).astype(BF16)
                mixed[half, rows, :] = (
                    jnp.dot(mix, perturb, preferred_element_type=F32) + mean_state
                )

        def narrow(step, carry):
            to = lax.rem(me + 5 * step, GROUP)
            for m in range(SHARE):
                block = jnp.concatenate(
                    [
                        mixed[half, pl.ds(to * SHARE + m, 4, stride=ENS), :]
                        for half in range(2)
                    ],
                    axis=1,
                )
                back[p, to, m] = block.astype(BF16)

            @pl.when(step > 0)
            def _():
                pltpu.make_async_remote_copy(
                    src_ref=back.at[p, to],
                    dst_ref=out.at[me * SHARE + p],
                    send_sem=back_send,
                    recv_sem=back_recv,
                    device_id={"mem": to},
                    device_id_type=MESH,
                ).start()

            @pl.when(step == 0)
            def _():
                pltpu.make_async_copy(
                    back.at[p, me], out.at[me * SHARE + p], back_own.at[p]
                ).start()

            return carry

        lax.fori_loop(0, GROUP, narrow, 0)
        return carry

    lax.fori_loop(0, SHARE, analyse, 0)

    others = (GROUP - 1) * SHARE
    msg_all.wait_send()
    for ref, send in ((state, state_send), (out, back_send)):
        whole = pltpu.make_async_remote_copy(
            src_ref=ref.at[pl.ds(0, others)],
            dst_ref=out.at[pl.ds(0, others)],
            send_sem=send,
            recv_sem=back_recv,
            device_id={"mem": lax.rem(me + 1, GROUP)},
            device_id_type=MESH,
        )
        whole.wait_send()
    whole.wait_recv()
    for p in range(SHARE):
        pltpu.make_async_copy(back.at[p, me], out.at[me * SHARE + p], back_own.at[p]).wait()


def body(state, obs_ens, obs_values, obs_index, patch_count, slot_weight):
    vmem, dma = pltpu.VMEM, pltpu.SemaphoreType.DMA
    block = state.shape[1:]
    scratch = [
        vmem(obs_ens.shape, F32),
        vmem(obs_values.shape, F32),
        vmem((8,) + obs_ens.shape[:3] + (RIM,), F32),
        vmem((8,) + obs_values.shape[:3] + (RIM,), F32),
        vmem(obs_index.shape, jnp.int32),
        vmem((SHARE, SLOTS), F32),
        vmem(patch_count.shape, jnp.int32),
        vmem((CHUNKS * 8, CHUNK), BF16),
        vmem((CHUNKS, CHUNK), F32),
        vmem((CHUNKS * 2, CHUNK), BF16),
        vmem((CHUNKS * 8, CHUNK), BF16),
        vmem((SHARE, SLOTS), F32),
        vmem((SHARE, SLOTS), F32),
        vmem((GROUP, MSG, SLOTS), BF16),
        vmem((GROUP, MSG, SLOTS), BF16),
        vmem((SHARE, GROUP) + block, BF16),
        vmem((SHARE, 2 * ENS, ENS), F32),
        vmem((SHARE, 8, SLOTS), F32),
        vmem((SHARE, 8, SLOTS), F32),
        vmem((SHARE, ENS, ENS), BF16),
        vmem((2, 4 * ENS, 128), F32),
        vmem((2, 4 * ENS, 128), F32),
        vmem((SHARE, GROUP) + block, BF16),
        dma((5,)),
        dma((8,)), dma((8,)), dma((8,)), dma((8,)),
        dma, dma, dma,
        dma, dma((SHARE,)), dma((SHARE,)),
        dma, dma, dma((SHARE,)),
    ]
    return pl.pallas_call(
        kernel,
        out_shape=jax.ShapeDtypeStruct(state.shape, state.dtype),
        in_specs=[pl.BlockSpec(memory_space=pl.ANY)] * 6,
        out_specs=pl.BlockSpec(memory_space=pl.ANY),
        scratch_shapes=scratch,
        compiler_params=pltpu.CompilerParams(
            collective_id=0, has_side_effects=True, vmem_limit_bytes=40 * 2**20
        ),
        name="letkf",
    )(state, obs_ens, obs_values, obs_index, patch_count, slot_weight)


def solution(mesh):
    placed = (
        P(("gx", "gy"), "mem", None, None),
        P("mem", "gx", "gy", None),
        P(None, "gx", "gy", None),
        P(("gx", "gy"), None),
        P(("gx", "gy")),
        P(("gx", "gy"), None),
    )
    return jax.shard_map(
        body,
        mesh=mesh,
        in_specs=placed,
        out_specs=P(("gx", "gy"), "mem", None, None),
        check_vma=False,
    )
```

```python
import math

import jax
import jax.numpy as jnp
from jax import lax
from jax.experimental import pallas as pl
from jax.experimental.pallas import tpu as pltpu
from jax.sharding import PartitionSpec as P

NS = 6
MESH = pl.DeviceIdType.MESH
F32 = jnp.float32
BF16 = jnp.bfloat16

GROUP = 16
SHARE = 8
SLOTS = 128
ENS = GROUP * SHARE
PATCHES = GROUP * SHARE
OBS = 8192
RIM = 2048
CHUNK = 256
OWN_CHUNKS = OBS // CHUNK
RIM_CHUNKS = RIM // CHUNK
CHUNKS = OWN_CHUNKS + 8 * RIM_CHUNKS
MSG = SHARE + 1
HOLD = 5
EARLY = 3

SIDES = [(dx, dy) for dx in (-1, 0, 1) for dy in (-1, 0, 1) if (dx, dy) != (0, 0)]


def split(a):
    high = a.astype(BF16)
    return high, (a - high.astype(F32)).astype(BF16)


def mm(a, b):
    a_high, a_low = split(a)
    b_high, b_low = split(b)
    row = jnp.concatenate([b_high, b_low], axis=1)
    out = jnp.dot(
        jnp.concatenate([a_high, a_low], axis=1),
        jnp.concatenate([row, row], axis=0),
        preferred_element_type=F32,
    )
    width = b.shape[1]
    return out[:, :width] + out[:, width:]


def mm_t(a, b):
    a_high, a_low = split(a)
    b_high, b_low = split(b)
    out = lax.dot_general(
        jnp.concatenate([a_high, a_low], axis=1),
        jnp.concatenate(
            [
                jnp.concatenate([b_high, b_high], axis=1),
                jnp.concatenate([b_low, b_low], axis=1),
            ],
            axis=0,
        ),
        (((1,), (1,)), ((), ())),
        preferred_element_type=F32,
    )
    width = b.shape[0]
    return out[:, :width] + out[:, width:]


def kernel(
    state, ens, vals, index, counts, weights, out,
    ens_raw, vals_raw, ens_rim, vals_rim, index_v, weights_v, counts_v,
    pool, mean_f, mean_pool, val_pool, obs_own, rate_own,
    msg_out, msg_in, state_in, root, pulled_s, frob_s, trans, wide, mixed, back,
    local_sem, rim_send, rim_recv, val_send, val_recv,
    msg_send, msg_recv, msg_own, state_send, state_recv, state_own,
    back_send, back_recv, back_own,
):
    me = lax.axis_index("mem")
    tile_x = lax.axis_index("gx")
    tile_y = lax.axis_index("gy")

    loads = [
        pltpu.make_async_copy(ens, ens_raw, local_sem.at[0]),
        pltpu.make_async_copy(vals, vals_raw, local_sem.at[1]),
        pltpu.make_async_copy(index, index_v, local_sem.at[2]),
        pltpu.make_async_copy(
            weights.at[pl.ds(pl.multiple_of(me * SHARE, SHARE), SHARE)],
            weights_v, local_sem.at[3],
        ),
        pltpu.make_async_copy(counts, counts_v, local_sem.at[4]),
    ]

    def tile_at(dx, dy):
        return {
            "gx": lax.rem(tile_x + dx + 4, 4),
            "gy": lax.rem(tile_y + dy + 4, 4),
        }

    barrier = pltpu.get_barrier_semaphore()
    for step in range(1, GROUP):
        pl.semaphore_signal(
            barrier, inc=1, device_id={"mem": lax.rem(me + step, GROUP)}, device_id_type=MESH
        )
    for dx, dy in SIDES:
        pl.semaphore_signal(barrier, inc=1, device_id=tile_at(dx, dy), device_id_type=MESH)

    def own_state(patch):
        return pltpu.make_async_copy(
            state.at[me * SHARE + patch], state_in.at[patch, me], state_own.at[patch]
        )

    def send_state(patch):
        def one(step, carry):
            to = lax.rem(me + 5 * step, GROUP)
            pltpu.make_async_remote_copy(
                src_ref=state.at[to * SHARE + patch],
                dst_ref=state_in.at[patch, me],
                send_sem=state_send,
                recv_sem=state_recv.at[patch],
                device_id={"mem": to},
                device_id_type=MESH,
            ).start()
            return carry

        lax.fori_loop(1, GROUP, one, 0)

    pl.semaphore_wait(barrier, len(SIDES) + GROUP - 1)
    send_state(0)
    for load in loads:
        load.start()
    for patch in range(SHARE):
        own_state(patch).start()

    loads[0].wait()
    loads[1].wait()
    rims = []
    for side, (dx, dy) in enumerate(SIDES):
        slot = len(SIDES) - 1 - side
        for src, dst, send, recv in (
            (ens_raw, ens_rim, rim_send, rim_recv),
            (vals_raw, vals_rim, val_send, val_recv),
        ):
            copy = pltpu.make_async_remote_copy(
                src_ref=src.at[:, :, :, pl.ds(0, RIM)],
                dst_ref=dst.at[slot],
                send_sem=send.at[slot],
                recv_sem=recv.at[slot],
                device_id=tile_at(dx, dy),
                device_id_type=MESH,
            )
            copy.start()
            rims.append(copy)

    for patch in range(1, EARLY):
        send_state(patch)

    def fill(chunk_pair, ens_block, vals_block):
        mean = jnp.mean(ens_block, axis=0, keepdims=True).astype(BF16).astype(F32)
        dev = ens_block - mean
        rows = pl.ds(pl.multiple_of(chunk_pair * 16, 16), 16)
        pool[rows, :] = jnp.concatenate([dev[:, :CHUNK], dev[:, CHUNK:]], axis=0).astype(BF16)
        mean_f[pl.ds(chunk_pair * 2, 1), :] = mean[:, :CHUNK]
        mean_f[pl.ds(chunk_pair * 2 + 1, 1), :] = mean[:, CHUNK:]
        first = vals_block.astype(BF16).astype(F32)
        rest = vals_block - first
        second = rest.astype(BF16).astype(F32)
        parts = jnp.concatenate([first, second, rest - second, jnp.zeros_like(first)], axis=0)
        val_pool[rows, :] = jnp.concatenate(
            [parts[:, :CHUNK], parts[:, CHUNK:]], axis=0
        ).astype(BF16)

    def fill_own(pair, carry):
        cols = pl.ds(pl.multiple_of(pair * 2 * CHUNK, 2 * CHUNK), 2 * CHUNK)
        fill(
            pair,
            jnp.concatenate([ens_raw[m, 0, :, cols] for m in range(SHARE)], axis=0),
            jnp.concatenate([vals_raw[c, 0, :, cols] for c in range(2)], axis=0),
        )
        return carry

    lax.fori_loop(0, OWN_CHUNKS // 2, fill_own, 0)

    for copy in rims:
        copy.wait()

    def fill_rim(step, carry):
        side = step // (RIM_CHUNKS // 2)
        pair = step % (RIM_CHUNKS // 2)
        cols = pl.ds(pl.multiple_of(pair * 2 * CHUNK, 2 * CHUNK), 2 * CHUNK)
        fill(
            OWN_CHUNKS // 2 + step,
            jnp.concatenate([ens_rim[side, m, 0, :, cols] for m in range(SHARE)], axis=0),
            jnp.concatenate([vals_rim[side, c, 0, :, cols] for c in range(2)], axis=0),
        )
        return carry

    lax.fori_loop(0, 8 * RIM_CHUNKS // 2, fill_rim, 0)
    mean_pool[...] = mean_f[...].astype(BF16)

    for load in loads[2:]:
        load.wait()

    sub_iota = lax.broadcasted_iota(jnp.int32, (CHUNK, 2 * SLOTS), 0)
    row_iota = lax.broadcasted_iota(jnp.int32, (8, 2 * SLOTS), 0)

    def pick(table, chunk_of, onehot):
        found = jnp.zeros((8, 2 * SLOTS), F32)
        for block in range(CHUNKS // 16):
            rows = jnp.dot(
                table[block * 128 : (block + 1) * 128, :], onehot, preferred_element_type=F32
            )
            for c in range(16):
                found = jnp.where(chunk_of == block * 16 + c, rows[8 * c : 8 * c + 8], found)
        return found

    def gather(step, carry):
        to = lax.rem(me + 5 * (step + 1), GROUP)
        codes = index_v[pl.ds(pl.multiple_of(to * SHARE, SHARE), SHARE), :]
        tile = codes >> 13
        pos = codes & (OBS - 1)
        side = jnp.where(tile > 4, tile - 1, tile)
        chunk = jnp.where(tile == 4, pos >> 8, OWN_CHUNKS + side * RIM_CHUNKS + (pos >> 8))
        lane = pos & (CHUNK - 1)
        pairs = []
        for pair in range(SHARE // 2):
            two = lambda a: jnp.concatenate(
                [a[2 * pair : 2 * pair + 1], a[2 * pair + 1 : 2 * pair + 2]], axis=1
            )
            onehot = jnp.where(sub_iota == two(lane), 1.0, 0.0).astype(BF16)
            pairs.append((onehot, jnp.broadcast_to(two(chunk), (8, 2 * SLOTS))))
        heads = []
        for pair, (onehot, chunk_of) in enumerate(pairs):
            dev = pick(pool, chunk_of, onehot)
            msg_out[step, 2 * pair] = dev[:, :SLOTS].astype(BF16)
            msg_out[step, 2 * pair + 1] = dev[:, SLOTS:].astype(BF16)
            rows = jnp.dot(mean_pool[...], onehot, preferred_element_type=F32)
            turned = chunk_of - row_iota
            found = jnp.zeros((8, 2 * SLOTS), F32)
            for k in range(CHUNKS // 8):
                found = jnp.where(turned == 8 * k, rows[8 * k : 8 * k + 8], found)
            found = jnp.sum(found, axis=0, keepdims=True)
            heads.extend([found[:, :SLOTS], found[:, SLOTS:]])
        msg_out[step, SHARE] = jnp.concatenate(heads, axis=0).astype(BF16)

        @pl.when(step < GROUP - 1)
        def _():
            pltpu.make_async_remote_copy(
                src_ref=msg_out.at[step],
                dst_ref=msg_in.at[me],
                send_sem=msg_send,
                recv_sem=msg_recv,
                device_id={"mem": to},
                device_id_type=MESH,
            ).start()

        @pl.when(step == GROUP - 1)
        def _():
            pltpu.make_async_copy(msg_out.at[step], msg_in.at[me], msg_own).start()
            for pair, (onehot, chunk_of) in enumerate(pairs):
                got = pick(val_pool, chunk_of, onehot)
                got = got[0:2] + got[2:4] + got[4:6]
                obs_own[2 * pair : 2 * pair + 1, :] = got[0:1, :SLOTS]
                obs_own[2 * pair + 1 : 2 * pair + 2, :] = got[0:1, SLOTS:]
                rate_own[2 * pair : 2 * pair + 1, :] = got[1:2, :SLOTS]
                rate_own[2 * pair + 1 : 2 * pair + 2, :] = got[1:2, SLOTS:]

        return carry

    lax.fori_loop(0, GROUP, gather, 0)

    for patch in range(EARLY, SHARE):
        send_state(patch)

    msg_all = pltpu.make_async_remote_copy(
        src_ref=msg_out.at[pl.ds(0, GROUP - 1)],
        dst_ref=msg_in.at[pl.ds(0, GROUP - 1)],
        send_sem=msg_send,
        recv_sem=msg_recv,
        device_id={"mem": lax.rem(me + 1, GROUP)},
        device_id_type=MESH,
    )
    msg_all.wait_recv()
    pltpu.make_async_copy(msg_out.at[GROUP - 1], msg_in.at[me], msg_own).wait()

    eye = jnp.where(
        lax.broadcasted_iota(jnp.int32, (ENS, ENS), 0)
        == lax.broadcasted_iota(jnp.int32, (ENS, ENS), 1),
        1.0,
        0.0,
    ).astype(F32)
    lane_iota = lax.broadcasted_iota(jnp.int32, (1, SLOTS), 1)
    counts_row = counts_v[...].reshape(1, PATCHES).astype(F32)
    for p in range(SHARE):
        dev = msg_in[:, p].astype(F32)
        head = msg_in[:, SHARE].astype(F32)[:, p : p + 1, :]
        chosen = (dev + head).reshape(ENS, SLOTS)
        mean_obs = jnp.mean(chosen, axis=0, keepdims=True)
        spread = chosen - mean_obs
        count = jnp.sum(
            jnp.where(lane_iota == me * SHARE + p, counts_row, 0.0), axis=1, keepdims=True
        )
        used = lane_iota.astype(F32) < count
        rate = jnp.where(used, rate_own[p : p + 1, :] * weights_v[p : p + 1, :], 0.0)
        misfit = obs_own[p : p + 1, :] - mean_obs
        system = mm_t(spread * rate, spread) + (ENS - 1.0) * eye
        square = jnp.sum(system * system, axis=1, keepdims=True)
        frob = jnp.sqrt(jnp.sum(square, axis=0, keepdims=True))
        pulled_s[p] = mm_t(jnp.broadcast_to(rate * misfit, (8, SLOTS)), spread)
        frob_s[p] = jnp.broadcast_to(frob, (8, SLOTS))
        scaled = system / frob
        change = 0.5 * (eye - scaled)
        root[p, :ENS] = eye + change
        root[p, ENS:] = scaled + mm(scaled, change)

    def sweep(step, carry):
        for p in range(SHARE):
            both = root[p]
            change = 0.5 * (eye - mm(both[:ENS], both[ENS:]))
            root[p] = both + mm(both, change)
        return carry

    lax.fori_loop(1, NS - 1, sweep, 0)
    for p in range(SHARE):
        both = root[p]
        inverse = both[:ENS]
        change = 0.5 * (eye - mm(inverse, both[ENS:]))
        inverse = inverse + mm(inverse, change)
        inv_half = inverse / jnp.sqrt(frob_s[p][0:1, :])
        shift = mm(mm(pulled_s[p], inv_half), inv_half)[0:1]
        trans[p] = (math.sqrt(ENS - 1.0) * inv_half + shift).astype(BF16)

    def analyse(p, carry):
        pltpu.make_async_remote_copy(
            src_ref=state.at[pl.ds(0, GROUP - 1)],
            dst_ref=state_in.at[p, pl.ds(0, GROUP - 1)],
            send_sem=state_send,
            recv_sem=state_recv.at[p],
            device_id={"mem": lax.rem(me + 1, GROUP)},
            device_id_type=MESH,
        ).wait_recv()
        own_state(p).wait()

        def widen(source, carry):
            for m in range(SHARE):
                block = state_in[p, source, m].astype(F32)
                for half in range(2):
                    wide[half, pl.ds(source * SHARE + m, 4, stride=ENS), :] = block[
                        :, 128 * half : 128 * half + 128
                    ]
            return carry

        lax.fori_loop(0, GROUP, widen, 0)
        mix = trans[p]
        for level in range(4):
            for half in range(2):
                rows = slice(ENS * level, ENS * level + ENS)
                block = wide[half, rows, :]
                mean_state = jnp.mean(block, axis=0, keepdims=True)
                perturb = (block - mean_state).astype(BF16)
                mixed[half, rows, :] = (
                    jnp.dot(mix, perturb, preferred_element_type=F32) + mean_state
                )

        def narrow(step, carry):
            to = lax.rem(me + 5 * step, GROUP)
            for m in range(SHARE):
                block = jnp.concatenate(
                    [
                        mixed[half, pl.ds(to * SHARE + m, 4, stride=ENS), :]
                        for half in range(2)
                    ],
                    axis=1,
                )
                back[p, to, m] = block.astype(BF16)

            @pl.when((step > 0) & (p < HOLD))
            def _():
                pltpu.make_async_remote_copy(
                    src_ref=back.at[p, to],
                    dst_ref=out.at[me * SHARE + p],
                    send_sem=back_send,
                    recv_sem=back_recv,
                    device_id={"mem": to},
                    device_id_type=MESH,
                ).start()

            @pl.when(step == 0)
            def _():
                pltpu.make_async_copy(
                    back.at[p, me], out.at[me * SHARE + p], back_own.at[p]
                ).start()

            return carry

        lax.fori_loop(0, GROUP, narrow, 0)
        return carry

    lax.fori_loop(0, SHARE, analyse, 0)

    def rest(step, carry):
        turn = step // 2
        chip = jnp.where(turn < 4, turn, 4 + lax.rem(me // 2 + turn, 4))
        to = chip * 2 + lax.rem(step, 2)

        @pl.when(to != me)
        def _():
            def one(p, carry):
                pltpu.make_async_remote_copy(
                    src_ref=back.at[p, to],
                    dst_ref=out.at[me * SHARE + p],
                    send_sem=back_send,
                    recv_sem=back_recv,
                    device_id={"mem": to},
                    device_id_type=MESH,
                ).start()
                return carry

            lax.fori_loop(HOLD, SHARE, one, 0)

        return carry

    lax.fori_loop(0, GROUP, rest, 0)

    others = (GROUP - 1) * SHARE
    msg_all.wait_send()
    for ref, send in ((state, state_send), (out, back_send)):
        whole = pltpu.make_async_remote_copy(
            src_ref=ref.at[pl.ds(0, others)],
            dst_ref=out.at[pl.ds(0, others)],
            send_sem=send,
            recv_sem=back_recv,
            device_id={"mem": lax.rem(me + 1, GROUP)},
            device_id_type=MESH,
        )
        whole.wait_send()
    whole.wait_recv()
    for p in range(SHARE):
        pltpu.make_async_copy(back.at[p, me], out.at[me * SHARE + p], back_own.at[p]).wait()


def body(state, obs_ens, obs_values, obs_index, patch_count, slot_weight):
    vmem, dma = pltpu.VMEM, pltpu.SemaphoreType.DMA
    block = state.shape[1:]
    scratch = [
        vmem(obs_ens.shape, F32),
        vmem(obs_values.shape, F32),
        vmem((8,) + obs_ens.shape[:3] + (RIM,), F32),
        vmem((8,) + obs_values.shape[:3] + (RIM,), F32),
        vmem(obs_index.shape, jnp.int32),
        vmem((SHARE, SLOTS), F32),
        vmem(patch_count.shape, jnp.int32),
        vmem((CHUNKS * 8, CHUNK), BF16),
        vmem((CHUNKS, CHUNK), F32),
        vmem((CHUNKS, CHUNK), BF16),
        vmem((CHUNKS * 8, CHUNK), BF16),
        vmem((SHARE, SLOTS), F32),
        vmem((SHARE, SLOTS), F32),
        vmem((GROUP, MSG, SHARE, SLOTS), BF16),
        vmem((GROUP, MSG, SHARE, SLOTS), BF16),
        vmem((SHARE, GROUP) + block, BF16),
        vmem((SHARE, 2 * ENS, ENS), F32),
        vmem((SHARE, 8, SLOTS), F32),
        vmem((SHARE, 8, SLOTS), F32),
        vmem((SHARE, ENS, ENS), BF16),
        vmem((2, 4 * ENS, 128), F32),
        vmem((2, 4 * ENS, 128), F32),
        vmem((SHARE, GROUP) + block, BF16),
        dma((5,)),
        dma((8,)), dma((8,)), dma((8,)), dma((8,)),
        dma, dma, dma,
        dma, dma((SHARE,)), dma((SHARE,)),
        dma, dma, dma((SHARE,)),
    ]
    return pl.pallas_call(
        kernel,
        out_shape=pltpu.VMEM(state.shape, state.dtype),
        in_specs=[pl.BlockSpec(memory_space=pl.ANY)] * 6,
        out_specs=pl.BlockSpec(memory_space=pltpu.VMEM),
        scratch_shapes=scratch,
        compiler_params=pltpu.CompilerParams(
            collective_id=0, has_side_effects=True, vmem_limit_bytes=40 * 2**20
        ),
        name="letkf",
    )(*[
        pltpu.with_memory_space_constraint(a, pltpu.HBM)
        for a in (state, obs_ens, obs_values, obs_index, patch_count, slot_weight)
    ])


def solution(mesh):
    placed = (
        P(("gx", "gy"), "mem", None, None),
        P("mem", "gx", "gy", None),
        P(None, "gx", "gy", None),
        P(("gx", "gy"), None),
        P(("gx", "gy")),
        P(("gx", "gy"), None),
    )
    return jax.shard_map(
        body,
        mesh=mesh,
        in_specs=placed,
        out_specs=P(("gx", "gy"), "mem", None, None),
        check_vma=False,
    )
```

```python
import math

import jax
import jax.numpy as jnp
from jax import lax
from jax.experimental import pallas as pl
from jax.experimental.pallas import tpu as pltpu
from jax.sharding import PartitionSpec as P

NS = 6
MESH = pl.DeviceIdType.MESH
F32 = jnp.float32
BF16 = jnp.bfloat16

GROUP = 16
SHARE = 8
SLOTS = 128
ENS = GROUP * SHARE
PATCHES = GROUP * SHARE
OBS = 8192
RIM = 2048
CHUNK = 256
OWN_CHUNKS = OBS // CHUNK
RIM_CHUNKS = RIM // CHUNK
CHUNKS = OWN_CHUNKS + 8 * RIM_CHUNKS
MSG = SHARE + 1
HOLD = 5
EARLY = 5

SIDES = [(dx, dy) for dx in (-1, 0, 1) for dy in (-1, 0, 1) if (dx, dy) != (0, 0)]


def split(a):
    high = a.astype(BF16)
    return high, (a - high.astype(F32)).astype(BF16)


def mm(a, b):
    a_high, a_low = split(a)
    b_high, b_low = split(b)
    row = jnp.concatenate([b_high, b_low], axis=1)
    out = jnp.dot(
        jnp.concatenate([a_high, a_low], axis=1),
        jnp.concatenate([row, row], axis=0),
        preferred_element_type=F32,
    )
    width = b.shape[1]
    return out[:, :width] + out[:, width:]


def mm_t(a, b):
    a_high, a_low = split(a)
    b_high, b_low = split(b)
    out = lax.dot_general(
        jnp.concatenate([a_high, a_low], axis=1),
        jnp.concatenate(
            [
                jnp.concatenate([b_high, b_high], axis=1),
                jnp.concatenate([b_low, b_low], axis=1),
            ],
            axis=0,
        ),
        (((1,), (1,)), ((), ())),
        preferred_element_type=F32,
    )
    width = b.shape[0]
    return out[:, :width] + out[:, width:]


def kernel(
    state, ens, vals, index, counts, weights, out,
    ens_raw, vals_raw, ens_rim, vals_rim, index_v, weights_v, counts_v,
    pool, mean_f, mean_pool, val_pool, obs_own, rate_own,
    msg_out, msg_in, state_in, root, pulled_s, frob_s, trans, wide, mixed, back,
    local_sem, rim_send, rim_recv, val_send, val_recv,
    msg_send, msg_recv, msg_own, state_send, state_recv, state_own,
    back_send, back_recv, back_own, ready, go,
):
    me = lax.axis_index("mem")
    tile_x = lax.axis_index("gx")
    tile_y = lax.axis_index("gy")

    loads = [
        pltpu.make_async_copy(ens, ens_raw, local_sem.at[0]),
        pltpu.make_async_copy(vals, vals_raw, local_sem.at[1]),
        pltpu.make_async_copy(index, index_v, local_sem.at[2]),
        pltpu.make_async_copy(
            weights.at[pl.ds(pl.multiple_of(me * SHARE, SHARE), SHARE)],
            weights_v, local_sem.at[3],
        ),
        pltpu.make_async_copy(counts, counts_v, local_sem.at[4]),
    ]

    def tile_at(dx, dy):
        return {
            "gx": lax.rem(tile_x + dx + 4, 4),
            "gy": lax.rem(tile_y + dy + 4, 4),
        }

    barrier = pltpu.get_barrier_semaphore()
    for step in range(1, GROUP):
        pl.semaphore_signal(
            barrier, inc=1, device_id={"mem": lax.rem(me + step, GROUP)}, device_id_type=MESH
        )
    @pl.when(me == 0)
    def _():
        for dx, dy in SIDES:
            pl.semaphore_signal(barrier, inc=1, device_id=tile_at(dx, dy), device_id_type=MESH)

    def own_state(patch):
        return pltpu.make_async_copy(
            state.at[me * SHARE + patch], state_in.at[patch, me], state_own.at[patch]
        )

    def send_state(patch):
        def one(step, carry):
            to = lax.rem(me + 5 * step, GROUP)
            pltpu.make_async_remote_copy(
                src_ref=state.at[to * SHARE + patch],
                dst_ref=state_in.at[patch, me],
                send_sem=state_send,
                recv_sem=state_recv.at[patch],
                device_id={"mem": to},
                device_id_type=MESH,
            ).start()
            return carry

        lax.fori_loop(1, GROUP, one, 0)

    pl.semaphore_wait(barrier, GROUP - 1 + jnp.where(me == 0, len(SIDES), 0))
    send_state(0)
    for load in loads:
        load.start()
    for patch in range(SHARE):
        own_state(patch).start()

    for patch in range(1, EARLY):
        send_state(patch)

    @pl.when(me == 0)
    def _():
        for dx, dy in SIDES:
            pl.semaphore_signal(ready, inc=1, device_id=tile_at(dx, dy), device_id_type=MESH)
        pl.semaphore_wait(ready, len(SIDES))
        for step in range(1, GROUP):
            pl.semaphore_signal(go, inc=1, device_id={"mem": step}, device_id_type=MESH)

    loads[0].wait()
    loads[1].wait()

    def fill(chunk_pair, ens_block, vals_block):
        mean = jnp.mean(ens_block, axis=0, keepdims=True).astype(BF16).astype(F32)
        dev = ens_block - mean
        rows = pl.ds(pl.multiple_of(chunk_pair * 16, 16), 16)
        pool[rows, :] = jnp.concatenate([dev[:, :CHUNK], dev[:, CHUNK:]], axis=0).astype(BF16)
        mean_f[pl.ds(chunk_pair * 2, 1), :] = mean[:, :CHUNK]
        mean_f[pl.ds(chunk_pair * 2 + 1, 1), :] = mean[:, CHUNK:]
        first = vals_block.astype(BF16).astype(F32)
        rest = vals_block - first
        second = rest.astype(BF16).astype(F32)
        parts = jnp.concatenate([first, second, rest - second, jnp.zeros_like(first)], axis=0)
        val_pool[rows, :] = jnp.concatenate(
            [parts[:, :CHUNK], parts[:, CHUNK:]], axis=0
        ).astype(BF16)

    def fill_own(pair, carry):
        cols = pl.ds(pl.multiple_of(pair * 2 * CHUNK, 2 * CHUNK), 2 * CHUNK)
        fill(
            pair,
            jnp.concatenate([ens_raw[m, 0, :, cols] for m in range(SHARE)], axis=0),
            jnp.concatenate([vals_raw[c, 0, :, cols] for c in range(2)], axis=0),
        )
        return carry

    lax.fori_loop(0, OWN_CHUNKS // 2, fill_own, 0)

    @pl.when(me != 0)
    def _():
        pl.semaphore_wait(go, 1)

    rims = []
    for side, (dx, dy) in enumerate(SIDES):
        slot = len(SIDES) - 1 - side
        for src, dst, send, recv in (
            (ens_raw, ens_rim, rim_send, rim_recv),
            (vals_raw, vals_rim, val_send, val_recv),
        ):
            copy = pltpu.make_async_remote_copy(
                src_ref=src.at[:, :, :, pl.ds(0, RIM)],
                dst_ref=dst.at[slot],
                send_sem=send.at[slot],
                recv_sem=recv.at[slot],
                device_id=tile_at(dx, dy),
                device_id_type=MESH,
            )
            copy.start()
            rims.append(copy)

    for copy in rims:
        copy.wait()

    def fill_rim(step, carry):
        side = step // (RIM_CHUNKS // 2)
        pair = step % (RIM_CHUNKS // 2)
        cols = pl.ds(pl.multiple_of(pair * 2 * CHUNK, 2 * CHUNK), 2 * CHUNK)
        fill(
            OWN_CHUNKS // 2 + step,
            jnp.concatenate([ens_rim[side, m, 0, :, cols] for m in range(SHARE)], axis=0),
            jnp.concatenate([vals_rim[side, c, 0, :, cols] for c in range(2)], axis=0),
        )
        return carry

    lax.fori_loop(0, 8 * RIM_CHUNKS // 2, fill_rim, 0)
    mean_pool[...] = mean_f[...].astype(BF16)

    for load in loads[2:]:
        load.wait()

    sub_iota = lax.broadcasted_iota(jnp.int32, (CHUNK, 2 * SLOTS), 0)
    row_iota = lax.broadcasted_iota(jnp.int32, (8, 2 * SLOTS), 0)

    def pick(table, chunk_of, onehot):
        found = jnp.zeros((8, 2 * SLOTS), F32)
        for block in range(CHUNKS // 16):
            rows = jnp.dot(
                table[block * 128 : (block + 1) * 128, :], onehot, preferred_element_type=F32
            )
            for c in range(16):
                found = jnp.where(chunk_of == block * 16 + c, rows[8 * c : 8 * c + 8], found)
        return found

    def gather(step, carry):
        to = lax.rem(me + 5 * (step + 1), GROUP)
        codes = index_v[pl.ds(pl.multiple_of(to * SHARE, SHARE), SHARE), :]
        tile = codes >> 13
        pos = codes & (OBS - 1)
        side = jnp.where(tile > 4, tile - 1, tile)
        chunk = jnp.where(tile == 4, pos >> 8, OWN_CHUNKS + side * RIM_CHUNKS + (pos >> 8))
        lane = pos & (CHUNK - 1)
        pairs = []
        for pair in range(SHARE // 2):
            two = lambda a: jnp.concatenate(
                [a[2 * pair : 2 * pair + 1], a[2 * pair + 1 : 2 * pair + 2]], axis=1
            )
            onehot = jnp.where(sub_iota == two(lane), 1.0, 0.0).astype(BF16)
            pairs.append((onehot, jnp.broadcast_to(two(chunk), (8, 2 * SLOTS))))
        heads = []
        for pair, (onehot, chunk_of) in enumerate(pairs):
            dev = pick(pool, chunk_of, onehot)
            msg_out[step, 2 * pair] = dev[:, :SLOTS].astype(BF16)
            msg_out[step, 2 * pair + 1] = dev[:, SLOTS:].astype(BF16)
            rows = jnp.dot(mean_pool[...], onehot, preferred_element_type=F32)
            turned = chunk_of - row_iota
            found = jnp.zeros((8, 2 * SLOTS), F32)
            for k in range(CHUNKS // 8):
                found = jnp.where(turned == 8 * k, rows[8 * k : 8 * k + 8], found)
            found = jnp.sum(found, axis=0, keepdims=True)
            heads.extend([found[:, :SLOTS], found[:, SLOTS:]])
        msg_out[step, SHARE] = jnp.concatenate(heads, axis=0).astype(BF16)

        @pl.when(step < GROUP - 1)
        def _():
            pltpu.make_async_remote_copy(
                src_ref=msg_out.at[step],
                dst_ref=msg_in.at[me],
                send_sem=msg_send,
                recv_sem=msg_recv,
                device_id={"mem": to},
                device_id_type=MESH,
            ).start()

        @pl.when(step == GROUP - 1)
        def _():
            pltpu.make_async_copy(msg_out.at[step], msg_in.at[me], msg_own).start()
            for pair, (onehot, chunk_of) in enumerate(pairs):
                got = pick(val_pool, chunk_of, onehot)
                got = got[0:2] + got[2:4] + got[4:6]
                obs_own[2 * pair : 2 * pair + 1, :] = got[0:1, :SLOTS]
                obs_own[2 * pair + 1 : 2 * pair + 2, :] = got[0:1, SLOTS:]
                rate_own[2 * pair : 2 * pair + 1, :] = got[1:2, :SLOTS]
                rate_own[2 * pair + 1 : 2 * pair + 2, :] = got[1:2, SLOTS:]

        return carry

    lax.fori_loop(0, GROUP, gather, 0)

    for patch in range(EARLY, SHARE):
        send_state(patch)

    msg_all = pltpu.make_async_remote_copy(
        src_ref=msg_out.at[pl.ds(0, GROUP - 1)],
        dst_ref=msg_in.at[pl.ds(0, GROUP - 1)],
        send_sem=msg_send,
        recv_sem=msg_recv,
        device_id={"mem": lax.rem(me + 1, GROUP)},
        device_id_type=MESH,
    )
    msg_all.wait_recv()
    pltpu.make_async_copy(msg_out.at[GROUP - 1], msg_in.at[me], msg_own).wait()

    eye = jnp.where(
        lax.broadcasted_iota(jnp.int32, (ENS, ENS), 0)
        == lax.broadcasted_iota(jnp.int32, (ENS, ENS), 1),
        1.0,
        0.0,
    ).astype(F32)
    lane_iota = lax.broadcasted_iota(jnp.int32, (1, SLOTS), 1)
    counts_row = counts_v[...].reshape(1, PATCHES).astype(F32)
    for p in range(SHARE):
        dev = msg_in[:, p].astype(F32)
        head = msg_in[:, SHARE].astype(F32)[:, p : p + 1, :]
        chosen = (dev + head).reshape(ENS, SLOTS)
        mean_obs = jnp.mean(chosen, axis=0, keepdims=True)
        spread = chosen - mean_obs
        count = jnp.sum(
            jnp.where(lane_iota == me * SHARE + p, counts_row, 0.0), axis=1, keepdims=True
        )
        used = lane_iota.astype(F32) < count
        rate = jnp.where(used, rate_own[p : p + 1, :] * weights_v[p : p + 1, :], 0.0)
        misfit = obs_own[p : p + 1, :] - mean_obs
        system = mm_t(spread * rate, spread) + (ENS - 1.0) * eye
        square = jnp.sum(system * system, axis=1, keepdims=True)
        frob = jnp.sqrt(jnp.sum(square, axis=0, keepdims=True))
        pulled_s[p] = mm_t(jnp.broadcast_to(rate * misfit, (8, SLOTS)), spread)
        frob_s[p] = jnp.broadcast_to(frob, (8, SLOTS))
        scaled = system / frob
        change = 0.5 * (eye - scaled)
        root[p, :ENS] = eye + change
        root[p, ENS:] = scaled + mm(scaled, change)

    def sweep(step, carry):
        for p in range(SHARE):
            both = root[p]
            change = 0.5 * (eye - mm(both[:ENS], both[ENS:]))
            root[p] = both + mm(both, change)
        return carry

    lax.fori_loop(1, NS - 1, sweep, 0)
    for p in range(SHARE):
        both = root[p]
        inverse = both[:ENS]
        change = 0.5 * (eye - mm(inverse, both[ENS:]))
        inverse = inverse + mm(inverse, change)
        inv_half = inverse / jnp.sqrt(frob_s[p][0:1, :])
        shift = mm(mm(pulled_s[p], inv_half), inv_half)[0:1]
        trans[p] = (math.sqrt(ENS - 1.0) * inv_half + shift).astype(BF16)

    def analyse(p, carry):
        pltpu.make_async_remote_copy(
            src_ref=state.at[pl.ds(0, GROUP - 1)],
            dst_ref=state_in.at[p, pl.ds(0, GROUP - 1)],
            send_sem=state_send,
            recv_sem=state_recv.at[p],
            device_id={"mem": lax.rem(me + 1, GROUP)},
            device_id_type=MESH,
        ).wait_recv()
        own_state(p).wait()

        def widen(source, carry):
            for m in range(SHARE):
                block = state_in[p, source, m].astype(F32)
                for half in range(2):
                    wide[half, pl.ds(source * SHARE + m, 4, stride=ENS), :] = block[
                        :, 128 * half : 128 * half + 128
                    ]
            return carry

        lax.fori_loop(0, GROUP, widen, 0)
        mix = trans[p]
        for level in range(4):
            for half in range(2):
                rows = slice(ENS * level, ENS * level + ENS)
                block = wide[half, rows, :]
                mean_state = jnp.mean(block, axis=0, keepdims=True)
                perturb = (block - mean_state).astype(BF16)
                mixed[half, rows, :] = (
                    jnp.dot(mix, perturb, preferred_element_type=F32) + mean_state
                )

        def narrow(step, carry):
            to = lax.rem(me + 5 * step, GROUP)
            for m in range(SHARE):
                block = jnp.concatenate(
                    [
                        mixed[half, pl.ds(to * SHARE + m, 4, stride=ENS), :]
                        for half in range(2)
                    ],
                    axis=1,
                )
                back[p, to, m] = block.astype(BF16)

            @pl.when((step > 0) & (p < HOLD))
            def _():
                pltpu.make_async_remote_copy(
                    src_ref=back.at[p, to],
                    dst_ref=out.at[me * SHARE + p],
                    send_sem=back_send,
                    recv_sem=back_recv,
                    device_id={"mem": to},
                    device_id_type=MESH,
                ).start()

            @pl.when(step == 0)
            def _():
                pltpu.make_async_copy(
                    back.at[p, me], out.at[me * SHARE + p], back_own.at[p]
                ).start()

            return carry

        lax.fori_loop(0, GROUP, narrow, 0)
        return carry

    lax.fori_loop(0, SHARE, analyse, 0)

    def rest(step, carry):
        turn = step // 2
        chip = jnp.where(turn < 4, turn, 4 + lax.rem(me // 2 + turn, 4))
        to = chip * 2 + lax.rem(step, 2)

        @pl.when(to != me)
        def _():
            def one(p, carry):
                pltpu.make_async_remote_copy(
                    src_ref=back.at[p, to],
                    dst_ref=out.at[me * SHARE + p],
                    send_sem=back_send,
                    recv_sem=back_recv,
                    device_id={"mem": to},
                    device_id_type=MESH,
                ).start()
                return carry

            lax.fori_loop(HOLD, SHARE, one, 0)

        return carry

    lax.fori_loop(0, GROUP, rest, 0)

    others = (GROUP - 1) * SHARE
    msg_all.wait_send()
    for ref, send in ((state, state_send), (out, back_send)):
        whole = pltpu.make_async_remote_copy(
            src_ref=ref.at[pl.ds(0, others)],
            dst_ref=out.at[pl.ds(0, others)],
            send_sem=send,
            recv_sem=back_recv,
            device_id={"mem": lax.rem(me + 1, GROUP)},
            device_id_type=MESH,
        )
        whole.wait_send()
    whole.wait_recv()
    for p in range(SHARE):
        pltpu.make_async_copy(back.at[p, me], out.at[me * SHARE + p], back_own.at[p]).wait()


def body(state, obs_ens, obs_values, obs_index, patch_count, slot_weight):
    vmem, dma = pltpu.VMEM, pltpu.SemaphoreType.DMA
    block = state.shape[1:]
    scratch = [
        vmem(obs_ens.shape, F32),
        vmem(obs_values.shape, F32),
        vmem((8,) + obs_ens.shape[:3] + (RIM,), F32),
        vmem((8,) + obs_values.shape[:3] + (RIM,), F32),
        vmem(obs_index.shape, jnp.int32),
        vmem((SHARE, SLOTS), F32),
        vmem(patch_count.shape, jnp.int32),
        vmem((CHUNKS * 8, CHUNK), BF16),
        vmem((CHUNKS, CHUNK), F32),
        vmem((CHUNKS, CHUNK), BF16),
        vmem((CHUNKS * 8, CHUNK), BF16),
        vmem((SHARE, SLOTS), F32),
        vmem((SHARE, SLOTS), F32),
        vmem((GROUP, MSG, SHARE, SLOTS), BF16),
        vmem((GROUP, MSG, SHARE, SLOTS), BF16),
        vmem((SHARE, GROUP) + block, BF16),
        vmem((SHARE, 2 * ENS, ENS), F32),
        vmem((SHARE, 8, SLOTS), F32),
        vmem((SHARE, 8, SLOTS), F32),
        vmem((SHARE, ENS, ENS), BF16),
        vmem((2, 4 * ENS, 128), F32),
        vmem((2, 4 * ENS, 128), F32),
        vmem((SHARE, GROUP) + block, BF16),
        dma((5,)),
        dma((8,)), dma((8,)), dma((8,)), dma((8,)),
        dma, dma, dma,
        dma, dma((SHARE,)), dma((SHARE,)),
        dma, dma, dma((SHARE,)),
        pltpu.SemaphoreType.REGULAR, pltpu.SemaphoreType.REGULAR,
    ]
    return pl.pallas_call(
        kernel,
        out_shape=pltpu.VMEM(state.shape, state.dtype),
        in_specs=[pl.BlockSpec(memory_space=pl.ANY)] * 6,
        out_specs=pl.BlockSpec(memory_space=pltpu.VMEM),
        scratch_shapes=scratch,
        compiler_params=pltpu.CompilerParams(
            collective_id=0, has_side_effects=True, vmem_limit_bytes=40 * 2**20
        ),
        name="letkf",
    )(*[
        pltpu.with_memory_space_constraint(a, pltpu.HBM)
        for a in (state, obs_ens, obs_values, obs_index, patch_count, slot_weight)
    ])


def solution(mesh):
    placed = (
        P(("gx", "gy"), "mem", None, None),
        P("mem", "gx", "gy", None),
        P(None, "gx", "gy", None),
        P(("gx", "gy"), None),
        P(("gx", "gy")),
        P(("gx", "gy"), None),
    )
    return jax.shard_map(
        body,
        mesh=mesh,
        in_specs=placed,
        out_specs=P(("gx", "gy"), "mem", None, None),
        check_vma=False,
    )
```

```python
import math

import jax
import jax.numpy as jnp
from jax import lax
from jax.experimental import pallas as pl
from jax.experimental.pallas import tpu as pltpu
from jax.sharding import PartitionSpec as P

NS = 6
MESH = pl.DeviceIdType.MESH
F32 = jnp.float32
BF16 = jnp.bfloat16

GROUP = 16
SHARE = 8
SLOTS = 128
ENS = GROUP * SHARE
PATCHES = GROUP * SHARE
OBS = 8192
RIM = 2048
CHUNK = 256
OWN_CHUNKS = OBS // CHUNK
RIM_CHUNKS = RIM // CHUNK
CHUNKS = OWN_CHUNKS + 8 * RIM_CHUNKS
MSG = SHARE + 1
HOLD = 5
EARLY = 5

SIDES = [(dx, dy) for dx in (-1, 0, 1) for dy in (-1, 0, 1) if (dx, dy) != (0, 0)]


def split(a):
    high = a.astype(BF16)
    return high, (a - high.astype(F32)).astype(BF16)


def mm(a, b):
    a_high, a_low = split(a)
    b_high, b_low = split(b)
    row = jnp.concatenate([b_high, b_low], axis=1)
    out = jnp.dot(
        jnp.concatenate([a_high, a_low], axis=1),
        jnp.concatenate([row, row], axis=0),
        preferred_element_type=F32,
    )
    width = b.shape[1]
    return out[:, :width] + out[:, width:]


def mm_t(a, b):
    a_high, a_low = split(a)
    b_high, b_low = split(b)
    out = lax.dot_general(
        jnp.concatenate([a_high, a_low], axis=1),
        jnp.concatenate(
            [
                jnp.concatenate([b_high, b_high], axis=1),
                jnp.concatenate([b_low, b_low], axis=1),
            ],
            axis=0,
        ),
        (((1,), (1,)), ((), ())),
        preferred_element_type=F32,
    )
    width = b.shape[0]
    return out[:, :width] + out[:, width:]


def kernel(
    state, ens, vals, index, counts, weights, out,
    ens_raw, vals_raw, ens_rim, vals_rim, index_v, weights_v, counts_v,
    pool, mean_f, mean_pool, val_pool, obs_own, rate_own,
    msg_out, msg_in, state_in, root, pulled_s, frob_s, trans, wide, mixed, back,
    local_sem, rim_send, rim_recv, val_send, val_recv,
    msg_send, msg_recv, msg_own, state_send, state_recv, state_own,
    back_send, back_recv, back_own, ready, go,
):
    me = lax.axis_index("mem")
    tile_x = lax.axis_index("gx")
    tile_y = lax.axis_index("gy")

    loads = [
        pltpu.make_async_copy(ens, ens_raw, local_sem.at[0]),
        pltpu.make_async_copy(vals, vals_raw, local_sem.at[1]),
        pltpu.make_async_copy(index, index_v, local_sem.at[2]),
        pltpu.make_async_copy(
            weights.at[pl.ds(pl.multiple_of(me * SHARE, SHARE), SHARE)],
            weights_v, local_sem.at[3],
        ),
        pltpu.make_async_copy(counts, counts_v, local_sem.at[4]),
    ]

    def tile_at(dx, dy):
        return {
            "gx": lax.rem(tile_x + dx + 4, 4),
            "gy": lax.rem(tile_y + dy + 4, 4),
        }

    barrier = pltpu.get_barrier_semaphore()
    for step in range(1, GROUP):
        pl.semaphore_signal(
            barrier, inc=1, device_id={"mem": lax.rem(me + step, GROUP)}, device_id_type=MESH
        )
    @pl.when(me == 0)
    def _():
        for dx, dy in SIDES:
            pl.semaphore_signal(barrier, inc=1, device_id=tile_at(dx, dy), device_id_type=MESH)

    def own_state(patch):
        return pltpu.make_async_copy(
            state.at[me * SHARE + patch], state_in.at[patch, me], state_own.at[patch]
        )

    def send_state(patch):
        def one(step, carry):
            to = lax.rem(me + 5 * step, GROUP)
            pltpu.make_async_remote_copy(
                src_ref=state.at[to * SHARE + patch],
                dst_ref=state_in.at[patch, me],
                send_sem=state_send,
                recv_sem=state_recv.at[patch],
                device_id={"mem": to},
                device_id_type=MESH,
            ).start()
            return carry

        lax.fori_loop(1, GROUP, one, 0)

    pl.semaphore_wait(barrier, GROUP - 1 + jnp.where(me == 0, len(SIDES), 0))
    send_state(0)
    for load in loads:
        load.start()
    for patch in range(SHARE):
        own_state(patch).start()

    send_state(1)

    @pl.when(me == 0)
    def _():
        for dx, dy in SIDES:
            pl.semaphore_signal(ready, inc=1, device_id=tile_at(dx, dy), device_id_type=MESH)
        pl.semaphore_wait(ready, len(SIDES))
        for step in range(1, GROUP):
            pl.semaphore_signal(go, inc=1, device_id={"mem": step}, device_id_type=MESH)

    loads[0].wait()
    loads[1].wait()

    def fill(chunk_pair, ens_block, vals_block):
        mean = jnp.mean(ens_block, axis=0, keepdims=True).astype(BF16).astype(F32)
        dev = ens_block - mean
        rows = pl.ds(pl.multiple_of(chunk_pair * 16, 16), 16)
        pool[rows, :] = jnp.concatenate([dev[:, :CHUNK], dev[:, CHUNK:]], axis=0).astype(BF16)
        mean_f[pl.ds(chunk_pair * 2, 1), :] = mean[:, :CHUNK]
        mean_f[pl.ds(chunk_pair * 2 + 1, 1), :] = mean[:, CHUNK:]
        first = vals_block.astype(BF16).astype(F32)
        rest = vals_block - first
        second = rest.astype(BF16).astype(F32)
        parts = jnp.concatenate([first, second, rest - second, jnp.zeros_like(first)], axis=0)
        val_pool[rows, :] = jnp.concatenate(
            [parts[:, :CHUNK], parts[:, CHUNK:]], axis=0
        ).astype(BF16)

    def fill_own(pair, carry):
        cols = pl.ds(pl.multiple_of(pair * 2 * CHUNK, 2 * CHUNK), 2 * CHUNK)
        fill(
            pair,
            jnp.concatenate([ens_raw[m, 0, :, cols] for m in range(SHARE)], axis=0),
            jnp.concatenate([vals_raw[c, 0, :, cols] for c in range(2)], axis=0),
        )
        return carry

    lax.fori_loop(0, OWN_CHUNKS // 2, fill_own, 0)

    @pl.when(me != 0)
    def _():
        pl.semaphore_wait(go, 1)

    rims = []
    for side, (dx, dy) in enumerate(SIDES):
        slot = len(SIDES) - 1 - side
        for src, dst, send, recv in (
            (ens_raw, ens_rim, rim_send, rim_recv),
            (vals_raw, vals_rim, val_send, val_recv),
        ):
            copy = pltpu.make_async_remote_copy(
                src_ref=src.at[:, :, :, pl.ds(0, RIM)],
                dst_ref=dst.at[slot],
                send_sem=send.at[slot],
                recv_sem=recv.at[slot],
                device_id=tile_at(dx, dy),
                device_id_type=MESH,
            )
            copy.start()
            rims.append(copy)

    for patch in range(2, EARLY):
        send_state(patch)

    for copy in rims:
        copy.wait()

    def fill_rim(step, carry):
        side = step // (RIM_CHUNKS // 2)
        pair = step % (RIM_CHUNKS // 2)
        cols = pl.ds(pl.multiple_of(pair * 2 * CHUNK, 2 * CHUNK), 2 * CHUNK)
        fill(
            OWN_CHUNKS // 2 + step,
            jnp.concatenate([ens_rim[side, m, 0, :, cols] for m in range(SHARE)], axis=0),
            jnp.concatenate([vals_rim[side, c, 0, :, cols] for c in range(2)], axis=0),
        )
        return carry

    lax.fori_loop(0, 8 * RIM_CHUNKS // 2, fill_rim, 0)
    mean_pool[...] = mean_f[...].astype(BF16)

    for load in loads[2:]:
        load.wait()

    sub_iota = lax.broadcasted_iota(jnp.int32, (CHUNK, 2 * SLOTS), 0)
    row_iota = lax.broadcasted_iota(jnp.int32, (8, 2 * SLOTS), 0)

    def pick(table, chunk_of, onehot):
        found = jnp.zeros((8, 2 * SLOTS), F32)
        for block in range(CHUNKS // 16):
            rows = jnp.dot(
                table[block * 128 : (block + 1) * 128, :], onehot, preferred_element_type=F32
            )
            for c in range(16):
                found = jnp.where(chunk_of == block * 16 + c, rows[8 * c : 8 * c + 8], found)
        return found

    def gather(step, carry):
        to = lax.rem(me + 5 * (step + 1), GROUP)
        codes = index_v[pl.ds(pl.multiple_of(to * SHARE, SHARE), SHARE), :]
        tile = codes >> 13
        pos = codes & (OBS - 1)
        side = jnp.where(tile > 4, tile - 1, tile)
        chunk = jnp.where(tile == 4, pos >> 8, OWN_CHUNKS + side * RIM_CHUNKS + (pos >> 8))
        lane = pos & (CHUNK - 1)
        pairs = []
        for pair in range(SHARE // 2):
            two = lambda a: jnp.concatenate(
                [a[2 * pair : 2 * pair + 1], a[2 * pair + 1 : 2 * pair + 2]], axis=1
            )
            onehot = jnp.where(sub_iota == two(lane), 1.0, 0.0).astype(BF16)
            pairs.append((onehot, jnp.broadcast_to(two(chunk), (8, 2 * SLOTS))))
        heads = []
        for pair, (onehot, chunk_of) in enumerate(pairs):
            dev = pick(pool, chunk_of, onehot)
            msg_out[step, 2 * pair] = dev[:, :SLOTS].astype(BF16)
            msg_out[step, 2 * pair + 1] = dev[:, SLOTS:].astype(BF16)
            rows = jnp.dot(mean_pool[...], onehot, preferred_element_type=F32)
            turned = chunk_of - row_iota
            found = jnp.zeros((8, 2 * SLOTS), F32)
            for k in range(CHUNKS // 8):
                found = jnp.where(turned == 8 * k, rows[8 * k : 8 * k + 8], found)
            found = jnp.sum(found, axis=0, keepdims=True)
            heads.extend([found[:, :SLOTS], found[:, SLOTS:]])
        msg_out[step, SHARE] = jnp.concatenate(heads, axis=0).astype(BF16)

        @pl.when(step < GROUP - 1)
        def _():
            pltpu.make_async_remote_copy(
                src_ref=msg_out.at[step],
                dst_ref=msg_in.at[me],
                send_sem=msg_send,
                recv_sem=msg_recv,
                device_id={"mem": to},
                device_id_type=MESH,
            ).start()

        @pl.when(step == GROUP - 1)
        def _():
            pltpu.make_async_copy(msg_out.at[step], msg_in.at[me], msg_own).start()
            for pair, (onehot, chunk_of) in enumerate(pairs):
                got = pick(val_pool, chunk_of, onehot)
                got = got[0:2] + got[2:4] + got[4:6]
                obs_own[2 * pair : 2 * pair + 1, :] = got[0:1, :SLOTS]
                obs_own[2 * pair + 1 : 2 * pair + 2, :] = got[0:1, SLOTS:]
                rate_own[2 * pair : 2 * pair + 1, :] = got[1:2, :SLOTS]
                rate_own[2 * pair + 1 : 2 * pair + 2, :] = got[1:2, SLOTS:]

        return carry

    lax.fori_loop(0, GROUP, gather, 0)

    for patch in range(EARLY, SHARE):
        send_state(patch)

    msg_all = pltpu.make_async_remote_copy(
        src_ref=msg_out.at[pl.ds(0, GROUP - 1)],
        dst_ref=msg_in.at[pl.ds(0, GROUP - 1)],
        send_sem=msg_send,
        recv_sem=msg_recv,
        device_id={"mem": lax.rem(me + 1, GROUP)},
        device_id_type=MESH,
    )
    msg_all.wait_recv()
    pltpu.make_async_copy(msg_out.at[GROUP - 1], msg_in.at[me], msg_own).wait()

    eye = jnp.where(
        lax.broadcasted_iota(jnp.int32, (ENS, ENS), 0)
        == lax.broadcasted_iota(jnp.int32, (ENS, ENS), 1),
        1.0,
        0.0,
    ).astype(F32)
    lane_iota = lax.broadcasted_iota(jnp.int32, (1, SLOTS), 1)
    counts_row = counts_v[...].reshape(1, PATCHES).astype(F32)
    for p in range(SHARE):
        dev = msg_in[:, p].astype(F32)
        head = msg_in[:, SHARE].astype(F32)[:, p : p + 1, :]
        chosen = (dev + head).reshape(ENS, SLOTS)
        mean_obs = jnp.mean(chosen, axis=0, keepdims=True)
        spread = chosen - mean_obs
        count = jnp.sum(
            jnp.where(lane_iota == me * SHARE + p, counts_row, 0.0), axis=1, keepdims=True
        )
        used = lane_iota.astype(F32) < count
        rate = jnp.where(used, rate_own[p : p + 1, :] * weights_v[p : p + 1, :], 0.0)
        misfit = obs_own[p : p + 1, :] - mean_obs
        system = mm_t(spread * rate, spread) + (ENS - 1.0) * eye
        square = jnp.sum(system * system, axis=1, keepdims=True)
        frob = jnp.sqrt(jnp.sum(square, axis=0, keepdims=True))
        pulled_s[p] = mm_t(jnp.broadcast_to(rate * misfit, (8, SLOTS)), spread)
        frob_s[p] = jnp.broadcast_to(frob, (8, SLOTS))
        scaled = system / frob
        change = 0.5 * (eye - scaled)
        root[p, :ENS] = eye + change
        root[p, ENS:] = scaled + mm(scaled, change)

    def sweep(step, carry):
        for p in range(SHARE):
            both = root[p]
            change = 0.5 * (eye - mm(both[:ENS], both[ENS:]))
            root[p] = both + mm(both, change)
        return carry

    lax.fori_loop(1, NS - 1, sweep, 0)
    for p in range(SHARE):
        both = root[p]
        inverse = both[:ENS]
        change = 0.5 * (eye - mm(inverse, both[ENS:]))
        inverse = inverse + mm(inverse, change)
        inv_half = inverse / jnp.sqrt(frob_s[p][0:1, :])
        shift = mm(mm(pulled_s[p], inv_half), inv_half)[0:1]
        trans[p] = (math.sqrt(ENS - 1.0) * inv_half + shift).astype(BF16)

    def analyse(p, carry):
        pltpu.make_async_remote_copy(
            src_ref=state.at[pl.ds(0, GROUP - 1)],
            dst_ref=state_in.at[p, pl.ds(0, GROUP - 1)],
            send_sem=state_send,
            recv_sem=state_recv.at[p],
            device_id={"mem": lax.rem(me + 1, GROUP)},
            device_id_type=MESH,
        ).wait_recv()
        own_state(p).wait()

        def widen(source, carry):
            for m in range(SHARE):
                block = state_in[p, source, m].astype(F32)
                for half in range(2):
                    wide[half, pl.ds(source * SHARE + m, 4, stride=ENS), :] = block[
                        :, 128 * half : 128 * half + 128
                    ]
            return carry

        lax.fori_loop(0, GROUP, widen, 0)
        mix = trans[p]
        for level in range(4):
            for half in range(2):
                rows = slice(ENS * level, ENS * level + ENS)
                block = wide[half, rows, :]
                mean_state = jnp.mean(block, axis=0, keepdims=True)
                perturb = (block - mean_state).astype(BF16)
                mixed[half, rows, :] = (
                    jnp.dot(mix, perturb, preferred_element_type=F32) + mean_state
                )

        def narrow(step, carry):
            to = lax.rem(me + 5 * step, GROUP)
            for m in range(SHARE):
                block = jnp.concatenate(
                    [
                        mixed[half, pl.ds(to * SHARE + m, 4, stride=ENS), :]
                        for half in range(2)
                    ],
                    axis=1,
                )
                back[p, to, m] = block.astype(BF16)

            @pl.when((step > 0) & (p < HOLD))
            def _():
                pltpu.make_async_remote_copy(
                    src_ref=back.at[p, to],
                    dst_ref=out.at[me * SHARE + p],
                    send_sem=back_send,
                    recv_sem=back_recv,
                    device_id={"mem": to},
                    device_id_type=MESH,
                ).start()

            @pl.when(step == 0)
            def _():
                pltpu.make_async_copy(
                    back.at[p, me], out.at[me * SHARE + p], back_own.at[p]
                ).start()

            return carry

        lax.fori_loop(0, GROUP, narrow, 0)
        return carry

    lax.fori_loop(0, SHARE, analyse, 0)

    def rest(step, carry):
        turn = step // 2
        chip = jnp.where(turn < 4, turn, 4 + lax.rem(me // 2 + turn, 4))
        to = chip * 2 + lax.rem(step, 2)

        @pl.when(to != me)
        def _():
            def one(p, carry):
                pltpu.make_async_remote_copy(
                    src_ref=back.at[p, to],
                    dst_ref=out.at[me * SHARE + p],
                    send_sem=back_send,
                    recv_sem=back_recv,
                    device_id={"mem": to},
                    device_id_type=MESH,
                ).start()
                return carry

            lax.fori_loop(HOLD, SHARE, one, 0)

        return carry

    lax.fori_loop(0, GROUP, rest, 0)

    others = (GROUP - 1) * SHARE
    msg_all.wait_send()
    for ref, send in ((state, state_send), (out, back_send)):
        whole = pltpu.make_async_remote_copy(
            src_ref=ref.at[pl.ds(0, others)],
            dst_ref=out.at[pl.ds(0, others)],
            send_sem=send,
            recv_sem=back_recv,
            device_id={"mem": lax.rem(me + 1, GROUP)},
            device_id_type=MESH,
        )
        whole.wait_send()
    whole.wait_recv()
    for p in range(SHARE):
        pltpu.make_async_copy(back.at[p, me], out.at[me * SHARE + p], back_own.at[p]).wait()


def body(state, obs_ens, obs_values, obs_index, patch_count, slot_weight):
    vmem, dma = pltpu.VMEM, pltpu.SemaphoreType.DMA
    block = state.shape[1:]
    scratch = [
        vmem(obs_ens.shape, F32),
        vmem(obs_values.shape, F32),
        vmem((8,) + obs_ens.shape[:3] + (RIM,), F32),
        vmem((8,) + obs_values.shape[:3] + (RIM,), F32),
        vmem(obs_index.shape, jnp.int32),
        vmem((SHARE, SLOTS), F32),
        vmem(patch_count.shape, jnp.int32),
        vmem((CHUNKS * 8, CHUNK), BF16),
        vmem((CHUNKS, CHUNK), F32),
        vmem((CHUNKS, CHUNK), BF16),
        vmem((CHUNKS * 8, CHUNK), BF16),
        vmem((SHARE, SLOTS), F32),
        vmem((SHARE, SLOTS), F32),
        vmem((GROUP, MSG, SHARE, SLOTS), BF16),
        vmem((GROUP, MSG, SHARE, SLOTS), BF16),
        vmem((SHARE, GROUP) + block, BF16),
        vmem((SHARE, 2 * ENS, ENS), F32),
        vmem((SHARE, 8, SLOTS), F32),
        vmem((SHARE, 8, SLOTS), F32),
        vmem((SHARE, ENS, ENS), BF16),
        vmem((2, 4 * ENS, 128), F32),
        vmem((2, 4 * ENS, 128), F32),
        vmem((SHARE, GROUP) + block, BF16),
        dma((5,)),
        dma((8,)), dma((8,)), dma((8,)), dma((8,)),
        dma, dma, dma,
        dma, dma((SHARE,)), dma((SHARE,)),
        dma, dma, dma((SHARE,)),
        pltpu.SemaphoreType.REGULAR, pltpu.SemaphoreType.REGULAR,
    ]
    return pl.pallas_call(
        kernel,
        out_shape=pltpu.VMEM(state.shape, state.dtype),
        in_specs=[pl.BlockSpec(memory_space=pl.ANY)] * 6,
        out_specs=pl.BlockSpec(memory_space=pltpu.VMEM),
        scratch_shapes=scratch,
        compiler_params=pltpu.CompilerParams(
            collective_id=0, has_side_effects=True, vmem_limit_bytes=40 * 2**20
        ),
        name="letkf",
    )(*[
        pltpu.with_memory_space_constraint(a, pltpu.HBM)
        for a in (state, obs_ens, obs_values, obs_index, patch_count, slot_weight)
    ])


def solution(mesh):
    placed = (
        P(("gx", "gy"), "mem", None, None),
        P("mem", "gx", "gy", None),
        P(None, "gx", "gy", None),
        P(("gx", "gy"), None),
        P(("gx", "gy")),
        P(("gx", "gy"), None),
    )
    return jax.shard_map(
        body,
        mesh=mesh,
        in_specs=placed,
        out_specs=P(("gx", "gy"), "mem", None, None),
        check_vma=False,
    )
```

```python
import math

import jax
import jax.numpy as jnp
from jax import lax
from jax.experimental import pallas as pl
from jax.experimental.pallas import tpu as pltpu
from jax.sharding import PartitionSpec as P

NS = 6
MESH = pl.DeviceIdType.MESH
F32 = jnp.float32
BF16 = jnp.bfloat16

GROUP = 16
SHARE = 8
SLOTS = 128
ENS = GROUP * SHARE
PATCHES = GROUP * SHARE
OBS = 8192
RIM = 2048
CHUNK = 256
OWN_CHUNKS = OBS // CHUNK
RIM_CHUNKS = RIM // CHUNK
CHUNKS = OWN_CHUNKS + 8 * RIM_CHUNKS
MSG = SHARE + 1
HOLD = 5
EARLY = 5

SIDES = [(dx, dy) for dx in (-1, 0, 1) for dy in (-1, 0, 1) if (dx, dy) != (0, 0)]


def split(a):
    high = a.astype(BF16)
    return high, (a - high.astype(F32)).astype(BF16)


def mm(a, b):
    a_high, a_low = split(a)
    b_high, b_low = split(b)
    row = jnp.concatenate([b_high, b_low], axis=1)
    out = jnp.dot(
        jnp.concatenate([a_high, a_low], axis=1),
        jnp.concatenate([row, row], axis=0),
        preferred_element_type=F32,
    )
    width = b.shape[1]
    return out[:, :width] + out[:, width:]


def mm_t(a, b):
    a_high, a_low = split(a)
    b_high, b_low = split(b)
    out = lax.dot_general(
        jnp.concatenate([a_high, a_low], axis=1),
        jnp.concatenate(
            [
                jnp.concatenate([b_high, b_high], axis=1),
                jnp.concatenate([b_low, b_low], axis=1),
            ],
            axis=0,
        ),
        (((1,), (1,)), ((), ())),
        preferred_element_type=F32,
    )
    width = b.shape[0]
    return out[:, :width] + out[:, width:]


def kernel(
    state, ens, vals, index, counts, weights, out,
    ens_raw, vals_raw, ens_rim, vals_rim, index_v, weights_v, counts_v,
    pool, mean_f, mean_pool, val_pool, obs_own, rate_own,
    msg_out, msg_in, state_in, root, pulled_s, frob_s, trans, wide, mixed, back,
    local_sem, rim_send, rim_recv, val_send, val_recv,
    msg_send, msg_recv, msg_own, state_send, state_recv, state_own,
    back_send, back_recv, back_own, ready, go,
):
    me = lax.axis_index("mem")
    tile_x = lax.axis_index("gx")
    tile_y = lax.axis_index("gy")

    loads = [
        pltpu.make_async_copy(ens, ens_raw, local_sem.at[0]),
        pltpu.make_async_copy(vals, vals_raw, local_sem.at[1]),
        pltpu.make_async_copy(index, index_v, local_sem.at[2]),
        pltpu.make_async_copy(
            weights.at[pl.ds(pl.multiple_of(me * SHARE, SHARE), SHARE)],
            weights_v, local_sem.at[3],
        ),
        pltpu.make_async_copy(counts, counts_v, local_sem.at[4]),
    ]

    def tile_at(dx, dy):
        return {
            "gx": lax.rem(tile_x + dx + 4, 4),
            "gy": lax.rem(tile_y + dy + 4, 4),
        }

    barrier = pltpu.get_barrier_semaphore()
    for step in range(1, GROUP):
        pl.semaphore_signal(
            barrier, inc=1, device_id={"mem": lax.rem(me + step, GROUP)}, device_id_type=MESH
        )
    @pl.when(me == 0)
    def _():
        for dx, dy in SIDES:
            pl.semaphore_signal(barrier, inc=1, device_id=tile_at(dx, dy), device_id_type=MESH)

    def own_state(patch):
        return pltpu.make_async_copy(
            state.at[me * SHARE + patch], state_in.at[patch, me], state_own.at[patch]
        )

    def send_state(patch):
        def one(step, carry):
            to = lax.rem(me + 5 * step, GROUP)
            pltpu.make_async_remote_copy(
                src_ref=state.at[to * SHARE + patch],
                dst_ref=state_in.at[patch, me],
                send_sem=state_send,
                recv_sem=state_recv.at[patch],
                device_id={"mem": to},
                device_id_type=MESH,
            ).start()
            return carry

        lax.fori_loop(1, GROUP, one, 0)

    pl.semaphore_wait(barrier, GROUP - 1 + jnp.where(me == 0, len(SIDES), 0))
    send_state(0)
    for load in loads:
        load.start()
    for patch in range(SHARE):
        own_state(patch).start()

    send_state(1)

    @pl.when(me == 0)
    def _():
        for dx, dy in SIDES:
            pl.semaphore_signal(ready, inc=1, device_id=tile_at(dx, dy), device_id_type=MESH)
        pl.semaphore_wait(ready, len(SIDES))
        for step in range(1, GROUP):
            pl.semaphore_signal(go, inc=1, device_id={"mem": step}, device_id_type=MESH)

    loads[0].wait()
    loads[1].wait()

    def fill(chunk_pair, ens_block, vals_block):
        mean = jnp.mean(ens_block, axis=0, keepdims=True).astype(BF16).astype(F32)
        dev = ens_block - mean
        rows = pl.ds(pl.multiple_of(chunk_pair * 16, 16), 16)
        pool[rows, :] = jnp.concatenate([dev[:, :CHUNK], dev[:, CHUNK:]], axis=0).astype(BF16)
        mean_f[pl.ds(chunk_pair * 2, 1), :] = mean[:, :CHUNK]
        mean_f[pl.ds(chunk_pair * 2 + 1, 1), :] = mean[:, CHUNK:]
        first = vals_block.astype(BF16).astype(F32)
        rest = vals_block - first
        second = rest.astype(BF16).astype(F32)
        parts = jnp.concatenate([first, second, rest - second, jnp.zeros_like(first)], axis=0)
        val_pool[rows, :] = jnp.concatenate(
            [parts[:, :CHUNK], parts[:, CHUNK:]], axis=0
        ).astype(BF16)

    def fill_own(pair, carry):
        cols = pl.ds(pl.multiple_of(pair * 2 * CHUNK, 2 * CHUNK), 2 * CHUNK)
        fill(
            pair,
            jnp.concatenate([ens_raw[m, 0, :, cols] for m in range(SHARE)], axis=0),
            jnp.concatenate([vals_raw[c, 0, :, cols] for c in range(2)], axis=0),
        )
        return carry

    lax.fori_loop(0, OWN_CHUNKS // 2, fill_own, 0)

    @pl.when(me != 0)
    def _():
        pl.semaphore_wait(go, 1)

    rims = []
    for side, (dx, dy) in enumerate(SIDES):
        slot = len(SIDES) - 1 - side
        for src, dst, send, recv in (
            (ens_raw, ens_rim, rim_send, rim_recv),
            (vals_raw, vals_rim, val_send, val_recv),
        ):
            copy = pltpu.make_async_remote_copy(
                src_ref=src.at[:, :, :, pl.ds(0, RIM)],
                dst_ref=dst.at[slot],
                send_sem=send.at[slot],
                recv_sem=recv.at[slot],
                device_id=tile_at(dx, dy),
                device_id_type=MESH,
            )
            copy.start()
            rims.append(copy)

    for patch in range(2, EARLY):
        send_state(patch)

    for copy in rims:
        copy.wait()

    def fill_rim(step, carry):
        side = step // (RIM_CHUNKS // 2)
        pair = step % (RIM_CHUNKS // 2)
        cols = pl.ds(pl.multiple_of(pair * 2 * CHUNK, 2 * CHUNK), 2 * CHUNK)
        fill(
            OWN_CHUNKS // 2 + step,
            jnp.concatenate([ens_rim[side, m, 0, :, cols] for m in range(SHARE)], axis=0),
            jnp.concatenate([vals_rim[side, c, 0, :, cols] for c in range(2)], axis=0),
        )
        return carry

    lax.fori_loop(0, 8 * RIM_CHUNKS // 2, fill_rim, 0)
    mean_pool[...] = mean_f[...].astype(BF16)

    for load in loads[2:]:
        load.wait()

    sub_iota = lax.broadcasted_iota(jnp.int32, (CHUNK, 2 * SLOTS), 0)
    row_iota = lax.broadcasted_iota(jnp.int32, (8, 2 * SLOTS), 0)

    def pick(table, chunk_of, onehot):
        found = jnp.zeros((8, 2 * SLOTS), F32)
        for block in range(CHUNKS // 16):
            rows = jnp.dot(
                table[block * 128 : (block + 1) * 128, :], onehot, preferred_element_type=F32
            )
            for c in range(16):
                found = jnp.where(chunk_of == block * 16 + c, rows[8 * c : 8 * c + 8], found)
        return found

    def gather(step, carry):
        to = lax.rem(me + 5 * (step + 1), GROUP)
        codes = index_v[pl.ds(pl.multiple_of(to * SHARE, SHARE), SHARE), :]
        tile = codes >> 13
        pos = codes & (OBS - 1)
        side = jnp.where(tile > 4, tile - 1, tile)
        chunk = jnp.where(tile == 4, pos >> 8, OWN_CHUNKS + side * RIM_CHUNKS + (pos >> 8))
        lane = pos & (CHUNK - 1)
        pairs = []
        for pair in range(SHARE // 2):
            two = lambda a: jnp.concatenate(
                [a[2 * pair : 2 * pair + 1], a[2 * pair + 1 : 2 * pair + 2]], axis=1
            )
            onehot = jnp.where(sub_iota == two(lane), 1.0, 0.0).astype(BF16)
            pairs.append((onehot, jnp.broadcast_to(two(chunk), (8, 2 * SLOTS))))
        heads = []
        for pair, (onehot, chunk_of) in enumerate(pairs):
            dev = pick(pool, chunk_of, onehot)
            msg_out[step, 2 * pair] = dev[:, :SLOTS].astype(BF16)
            msg_out[step, 2 * pair + 1] = dev[:, SLOTS:].astype(BF16)
            rows = jnp.dot(mean_pool[...], onehot, preferred_element_type=F32)
            turned = chunk_of - row_iota
            found = jnp.zeros((8, 2 * SLOTS), F32)
            for k in range(CHUNKS // 8):
                found = jnp.where(turned == 8 * k, rows[8 * k : 8 * k + 8], found)
            found = jnp.sum(found, axis=0, keepdims=True)
            heads.extend([found[:, :SLOTS], found[:, SLOTS:]])
        msg_out[step, SHARE] = jnp.concatenate(heads, axis=0).astype(BF16)

        @pl.when(step < GROUP - 1)
        def _():
            pltpu.make_async_remote_copy(
                src_ref=msg_out.at[step],
                dst_ref=msg_in.at[me],
                send_sem=msg_send,
                recv_sem=msg_recv,
                device_id={"mem": to},
                device_id_type=MESH,
            ).start()

        @pl.when(step == GROUP - 1)
        def _():
            pltpu.make_async_copy(msg_out.at[step], msg_in.at[me], msg_own).start()
            for pair, (onehot, chunk_of) in enumerate(pairs):
                got = pick(val_pool, chunk_of, onehot)
                got = got[0:2] + got[2:4] + got[4:6]
                obs_own[2 * pair : 2 * pair + 1, :] = got[0:1, :SLOTS]
                obs_own[2 * pair + 1 : 2 * pair + 2, :] = got[0:1, SLOTS:]
                rate_own[2 * pair : 2 * pair + 1, :] = got[1:2, :SLOTS]
                rate_own[2 * pair + 1 : 2 * pair + 2, :] = got[1:2, SLOTS:]

        return carry

    lax.fori_loop(0, GROUP, gather, 0)

    for patch in range(EARLY, SHARE):
        send_state(patch)

    msg_all = pltpu.make_async_remote_copy(
        src_ref=msg_out.at[pl.ds(0, GROUP - 1)],
        dst_ref=msg_in.at[pl.ds(0, GROUP - 1)],
        send_sem=msg_send,
        recv_sem=msg_recv,
        device_id={"mem": lax.rem(me + 1, GROUP)},
        device_id_type=MESH,
    )
    msg_all.wait_recv()
    pltpu.make_async_copy(msg_out.at[GROUP - 1], msg_in.at[me], msg_own).wait()

    eye = jnp.where(
        lax.broadcasted_iota(jnp.int32, (ENS, ENS), 0)
        == lax.broadcasted_iota(jnp.int32, (ENS, ENS), 1),
        1.0,
        0.0,
    ).astype(F32)
    lane_iota = lax.broadcasted_iota(jnp.int32, (1, SLOTS), 1)
    counts_row = counts_v[...].reshape(1, PATCHES).astype(F32)
    for p in range(SHARE):
        dev = msg_in[:, p].astype(F32)
        head = msg_in[:, SHARE].astype(F32)[:, p : p + 1, :]
        chosen = (dev + head).reshape(ENS, SLOTS)
        mean_obs = jnp.mean(chosen, axis=0, keepdims=True)
        spread = chosen - mean_obs
        count = jnp.sum(
            jnp.where(lane_iota == me * SHARE + p, counts_row, 0.0), axis=1, keepdims=True
        )
        used = lane_iota.astype(F32) < count
        rate = jnp.where(used, rate_own[p : p + 1, :] * weights_v[p : p + 1, :], 0.0)
        misfit = obs_own[p : p + 1, :] - mean_obs
        system = mm_t(spread * rate, spread) + (ENS - 1.0) * eye
        square = jnp.sum(system * system, axis=1, keepdims=True)
        frob = jnp.sqrt(jnp.sum(square, axis=0, keepdims=True))
        pulled_s[p] = mm_t(jnp.broadcast_to(rate * misfit, (8, SLOTS)), spread)
        frob_s[p] = jnp.broadcast_to(frob, (8, SLOTS))
        scaled = system / frob
        change = 0.5 * (eye - scaled)
        root[p, :ENS] = eye + change
        root[p, ENS:] = scaled + mm(scaled, change)

    def sweep(step, carry):
        for p in range(SHARE):
            both = root[p]
            change = 0.5 * (eye - mm(both[:ENS], both[ENS:]))
            root[p] = both + mm(both, change)
        return carry

    lax.fori_loop(1, NS - 1, sweep, 0)
    for p in range(SHARE):
        both = root[p]
        inverse = both[:ENS]
        change = 0.5 * (eye - mm(inverse, both[ENS:]))
        inverse = inverse + mm(inverse, change)
        inv_half = inverse / jnp.sqrt(frob_s[p][0:1, :])
        shift = mm(mm(pulled_s[p], inv_half), inv_half)[0:1]
        trans[p] = (math.sqrt(ENS - 1.0) * inv_half + shift).astype(BF16)

    def analyse(p, carry):
        pltpu.make_async_remote_copy(
            src_ref=state.at[pl.ds(0, GROUP - 1)],
            dst_ref=state_in.at[p, pl.ds(0, GROUP - 1)],
            send_sem=state_send,
            recv_sem=state_recv.at[p],
            device_id={"mem": lax.rem(me + 1, GROUP)},
            device_id_type=MESH,
        ).wait_recv()
        own_state(p).wait()

        def widen(source, carry):
            for m in range(SHARE):
                block = state_in[p, source, m].astype(F32)
                for half in range(2):
                    wide[half, pl.ds(source * SHARE + m, 4, stride=ENS), :] = block[
                        :, 128 * half : 128 * half + 128
                    ]
            return carry

        lax.fori_loop(0, GROUP, widen, 0)
        mix = trans[p]
        for level in range(4):
            for half in range(2):
                rows = slice(ENS * level, ENS * level + ENS)
                block = wide[half, rows, :]
                mean_state = jnp.mean(block, axis=0, keepdims=True)
                perturb = (block - mean_state).astype(BF16)
                mixed[half, rows, :] = (
                    jnp.dot(mix, perturb, preferred_element_type=F32) + mean_state
                )

        def narrow(step, carry):
            to = lax.rem(me + 5 * step, GROUP)
            for m in range(SHARE):
                block = jnp.concatenate(
                    [
                        mixed[half, pl.ds(to * SHARE + m, 4, stride=ENS), :]
                        for half in range(2)
                    ],
                    axis=1,
                )
                back[p, to, m] = block.astype(BF16)

            @pl.when((step > 0) & (p < HOLD))
            def _():
                pltpu.make_async_remote_copy(
                    src_ref=back.at[p, to],
                    dst_ref=out.at[me * SHARE + p],
                    send_sem=back_send,
                    recv_sem=back_recv,
                    device_id={"mem": to},
                    device_id_type=MESH,
                ).start()

            @pl.when(step == 0)
            def _():
                pltpu.make_async_copy(
                    back.at[p, me], out.at[me * SHARE + p], back_own.at[p]
                ).start()

            return carry

        lax.fori_loop(0, GROUP, narrow, 0)
        return carry

    lax.fori_loop(0, SHARE, analyse, 0)

    def rest(step, carry):
        turn = step // 2
        chip = jnp.where(turn < 4, turn, 4 + lax.rem(me // 2 + turn, 4))
        to = chip * 2 + 1 - lax.rem(step, 2)

        @pl.when(to != me)
        def _():
            def one(p, carry):
                pltpu.make_async_remote_copy(
                    src_ref=back.at[p, to],
                    dst_ref=out.at[me * SHARE + p],
                    send_sem=back_send,
                    recv_sem=back_recv,
                    device_id={"mem": to},
                    device_id_type=MESH,
                ).start()
                return carry

            lax.fori_loop(HOLD, SHARE, one, 0)

        return carry

    lax.fori_loop(0, GROUP, rest, 0)

    others = (GROUP - 1) * SHARE
    msg_all.wait_send()
    for ref, send in ((state, state_send), (out, back_send)):
        whole = pltpu.make_async_remote_copy(
            src_ref=ref.at[pl.ds(0, others)],
            dst_ref=out.at[pl.ds(0, others)],
            send_sem=send,
            recv_sem=back_recv,
            device_id={"mem": lax.rem(me + 1, GROUP)},
            device_id_type=MESH,
        )
        whole.wait_send()
    whole.wait_recv()
    for p in range(SHARE):
        pltpu.make_async_copy(back.at[p, me], out.at[me * SHARE + p], back_own.at[p]).wait()


def body(state, obs_ens, obs_values, obs_index, patch_count, slot_weight):
    vmem, dma = pltpu.VMEM, pltpu.SemaphoreType.DMA
    block = state.shape[1:]
    scratch = [
        vmem(obs_ens.shape, F32),
        vmem(obs_values.shape, F32),
        vmem((8,) + obs_ens.shape[:3] + (RIM,), F32),
        vmem((8,) + obs_values.shape[:3] + (RIM,), F32),
        vmem(obs_index.shape, jnp.int32),
        vmem((SHARE, SLOTS), F32),
        vmem(patch_count.shape, jnp.int32),
        vmem((CHUNKS * 8, CHUNK), BF16),
        vmem((CHUNKS, CHUNK), F32),
        vmem((CHUNKS, CHUNK), BF16),
        vmem((CHUNKS * 8, CHUNK), BF16),
        vmem((SHARE, SLOTS), F32),
        vmem((SHARE, SLOTS), F32),
        vmem((GROUP, MSG, SHARE, SLOTS), BF16),
        vmem((GROUP, MSG, SHARE, SLOTS), BF16),
        vmem((SHARE, GROUP) + block, BF16),
        vmem((SHARE, 2 * ENS, ENS), F32),
        vmem((SHARE, 8, SLOTS), F32),
        vmem((SHARE, 8, SLOTS), F32),
        vmem((SHARE, ENS, ENS), BF16),
        vmem((2, 4 * ENS, 128), F32),
        vmem((2, 4 * ENS, 128), F32),
        vmem((SHARE, GROUP) + block, BF16),
        dma((5,)),
        dma((8,)), dma((8,)), dma((8,)), dma((8,)),
        dma, dma, dma,
        dma, dma((SHARE,)), dma((SHARE,)),
        dma, dma, dma((SHARE,)),
        pltpu.SemaphoreType.REGULAR, pltpu.SemaphoreType.REGULAR,
    ]
    return pl.pallas_call(
        kernel,
        out_shape=pltpu.VMEM(state.shape, state.dtype),
        in_specs=[pl.BlockSpec(memory_space=pl.ANY)] * 6,
        out_specs=pl.BlockSpec(memory_space=pltpu.VMEM),
        scratch_shapes=scratch,
        compiler_params=pltpu.CompilerParams(
            collective_id=0, has_side_effects=True, vmem_limit_bytes=40 * 2**20
        ),
        name="letkf",
    )(*[
        pltpu.with_memory_space_constraint(a, pltpu.HBM)
        for a in (state, obs_ens, obs_values, obs_index, patch_count, slot_weight)
    ])


def solution(mesh):
    placed = (
        P(("gx", "gy"), "mem", None, None),
        P("mem", "gx", "gy", None),
        P(None, "gx", "gy", None),
        P(("gx", "gy"), None),
        P(("gx", "gy")),
        P(("gx", "gy"), None),
    )
    return jax.shard_map(
        body,
        mesh=mesh,
        in_specs=placed,
        out_specs=P(("gx", "gy"), "mem", None, None),
        check_vma=False,
    )
```

```python
import math

import jax
import jax.numpy as jnp
from jax import lax
from jax.experimental import pallas as pl
from jax.experimental.pallas import tpu as pltpu
from jax.sharding import PartitionSpec as P

NS = 6
MESH = pl.DeviceIdType.MESH
F32 = jnp.float32
BF16 = jnp.bfloat16

GROUP = 16
SHARE = 8
SLOTS = 128
ENS = GROUP * SHARE
PATCHES = GROUP * SHARE
OBS = 8192
RIM = 2048
CHUNK = 256
OWN_CHUNKS = OBS // CHUNK
RIM_CHUNKS = RIM // CHUNK
CHUNKS = OWN_CHUNKS + 8 * RIM_CHUNKS
MSG = SHARE + 1
HOLD = 5
EARLY = 5

SIDES = [(dx, dy) for dx in (-1, 0, 1) for dy in (-1, 0, 1) if (dx, dy) != (0, 0)]


def split(a):
    high = a.astype(BF16)
    return high, (a - high.astype(F32)).astype(BF16)


def mm(a, b):
    a_high, a_low = split(a)
    b_high, b_low = split(b)
    row = jnp.concatenate([b_high, b_low], axis=1)
    out = jnp.dot(
        jnp.concatenate([a_high, a_low], axis=1),
        jnp.concatenate([row, row], axis=0),
        preferred_element_type=F32,
    )
    width = b.shape[1]
    return out[:, :width] + out[:, width:]


def mm_t(a, b):
    a_high, a_low = split(a)
    b_high, b_low = split(b)
    out = lax.dot_general(
        jnp.concatenate([a_high, a_low], axis=1),
        jnp.concatenate(
            [
                jnp.concatenate([b_high, b_high], axis=1),
                jnp.concatenate([b_low, b_low], axis=1),
            ],
            axis=0,
        ),
        (((1,), (1,)), ((), ())),
        preferred_element_type=F32,
    )
    width = b.shape[0]
    return out[:, :width] + out[:, width:]


def kernel(
    state, ens, vals, index, counts, weights, out,
    ens_raw, vals_raw, ens_rim, vals_rim, index_v, weights_v, counts_v,
    pool, mean_f, mean_pool, val_pool, obs_own, rate_own,
    msg_out, msg_in, state_in, root, pulled_s, frob_s, trans, wide, mixed, back,
    local_sem, rim_send, rim_recv, val_send, val_recv,
    msg_send, msg_recv, msg_own, state_send, state_recv, state_own,
    back_send, back_recv, back_own, ready, go,
):
    me = lax.axis_index("mem")
    tile_x = lax.axis_index("gx")
    tile_y = lax.axis_index("gy")

    loads = [
        pltpu.make_async_copy(ens, ens_raw, local_sem.at[0]),
        pltpu.make_async_copy(vals, vals_raw, local_sem.at[1]),
        pltpu.make_async_copy(index, index_v, local_sem.at[2]),
        pltpu.make_async_copy(
            weights.at[pl.ds(pl.multiple_of(me * SHARE, SHARE), SHARE)],
            weights_v, local_sem.at[3],
        ),
        pltpu.make_async_copy(counts, counts_v, local_sem.at[4]),
    ]

    def tile_at(dx, dy):
        return {
            "gx": lax.rem(tile_x + dx + 4, 4),
            "gy": lax.rem(tile_y + dy + 4, 4),
        }

    barrier = pltpu.get_barrier_semaphore()
    for step in range(1, GROUP):
        pl.semaphore_signal(
            barrier, inc=1, device_id={"mem": lax.rem(me + step, GROUP)}, device_id_type=MESH
        )
    @pl.when(me == 0)
    def _():
        for dx, dy in SIDES:
            pl.semaphore_signal(barrier, inc=1, device_id=tile_at(dx, dy), device_id_type=MESH)

    def own_state(patch):
        return pltpu.make_async_copy(
            state.at[me * SHARE + patch], state_in.at[patch, me], state_own.at[patch]
        )

    def send_state(patch):
        def one(step, carry):
            to = lax.rem(me + 5 * step, GROUP)
            pltpu.make_async_remote_copy(
                src_ref=state.at[to * SHARE + patch],
                dst_ref=state_in.at[patch, me],
                send_sem=state_send,
                recv_sem=state_recv.at[patch],
                device_id={"mem": to},
                device_id_type=MESH,
            ).start()
            return carry

        lax.fori_loop(1, GROUP, one, 0)

    pl.semaphore_wait(barrier, GROUP - 1 + jnp.where(me == 0, len(SIDES), 0))
    send_state(0)
    for load in loads:
        load.start()
    for patch in range(SHARE):
        own_state(patch).start()

    send_state(1)

    @pl.when(me == 0)
    def _():
        for dx, dy in SIDES:
            pl.semaphore_signal(ready, inc=1, device_id=tile_at(dx, dy), device_id_type=MESH)
        pl.semaphore_wait(ready, len(SIDES))
        for step in range(1, GROUP):
            pl.semaphore_signal(go, inc=1, device_id={"mem": step}, device_id_type=MESH)

    loads[0].wait()
    loads[1].wait()

    def fill(chunk_pair, ens_block, vals_block):
        mean = jnp.mean(ens_block, axis=0, keepdims=True).astype(BF16).astype(F32)
        dev = ens_block - mean
        rows = pl.ds(pl.multiple_of(chunk_pair * 16, 16), 16)
        pool[rows, :] = jnp.concatenate([dev[:, :CHUNK], dev[:, CHUNK:]], axis=0).astype(BF16)
        mean_f[pl.ds(chunk_pair * 2, 1), :] = mean[:, :CHUNK]
        mean_f[pl.ds(chunk_pair * 2 + 1, 1), :] = mean[:, CHUNK:]
        first = vals_block.astype(BF16).astype(F32)
        rest = vals_block - first
        second = rest.astype(BF16).astype(F32)
        parts = jnp.concatenate([first, second, rest - second, jnp.zeros_like(first)], axis=0)
        val_pool[rows, :] = jnp.concatenate(
            [parts[:, :CHUNK], parts[:, CHUNK:]], axis=0
        ).astype(BF16)

    def fill_own(pair, carry):
        cols = pl.ds(pl.multiple_of(pair * 2 * CHUNK, 2 * CHUNK), 2 * CHUNK)
        fill(
            pair,
            jnp.concatenate([ens_raw[m, 0, :, cols] for m in range(SHARE)], axis=0),
            jnp.concatenate([vals_raw[c, 0, :, cols] for c in range(2)], axis=0),
        )
        return carry

    lax.fori_loop(0, OWN_CHUNKS // 2, fill_own, 0)

    @pl.when(me != 0)
    def _():
        pl.semaphore_wait(go, 1)

    rims = []
    for side, (dx, dy) in enumerate(SIDES):
        slot = len(SIDES) - 1 - side
        for src, dst, send, recv in (
            (ens_raw, ens_rim, rim_send, rim_recv),
            (vals_raw, vals_rim, val_send, val_recv),
        ):
            copy = pltpu.make_async_remote_copy(
                src_ref=src.at[:, :, :, pl.ds(0, RIM)],
                dst_ref=dst.at[slot],
                send_sem=send.at[slot],
                recv_sem=recv.at[slot],
                device_id=tile_at(dx, dy),
                device_id_type=MESH,
            )
            copy.start()
            rims.append(copy)

    for patch in range(2, EARLY):
        send_state(patch)

    for copy in rims:
        copy.wait()

    def fill_rim(step, carry):
        side = step // (RIM_CHUNKS // 2)
        pair = step % (RIM_CHUNKS // 2)
        cols = pl.ds(pl.multiple_of(pair * 2 * CHUNK, 2 * CHUNK), 2 * CHUNK)
        fill(
            OWN_CHUNKS // 2 + step,
            jnp.concatenate([ens_rim[side, m, 0, :, cols] for m in range(SHARE)], axis=0),
            jnp.concatenate([vals_rim[side, c, 0, :, cols] for c in range(2)], axis=0),
        )
        return carry

    lax.fori_loop(0, 8 * RIM_CHUNKS // 2, fill_rim, 0)
    mean_pool[...] = mean_f[...].astype(BF16)

    for load in loads[2:]:
        load.wait()

    sub_iota = lax.broadcasted_iota(jnp.int32, (CHUNK, 2 * SLOTS), 0)
    row_iota = lax.broadcasted_iota(jnp.int32, (8, 2 * SLOTS), 0)

    def pick(table, chunk_of, onehot):
        found = jnp.zeros((8, 2 * SLOTS), F32)
        for block in range(CHUNKS // 16):
            rows = jnp.dot(
                table[block * 128 : (block + 1) * 128, :], onehot, preferred_element_type=F32
            )
            for c in range(16):
                found = jnp.where(chunk_of == block * 16 + c, rows[8 * c : 8 * c + 8], found)
        return found

    def gather(step, carry):
        to = lax.rem(me + 5 * (step + 1), GROUP)
        codes = index_v[pl.ds(pl.multiple_of(to * SHARE, SHARE), SHARE), :]
        tile = codes >> 13
        pos = codes & (OBS - 1)
        side = jnp.where(tile > 4, tile - 1, tile)
        chunk = jnp.where(tile == 4, pos >> 8, OWN_CHUNKS + side * RIM_CHUNKS + (pos >> 8))
        lane = pos & (CHUNK - 1)
        pairs = []
        for pair in range(SHARE // 2):
            two = lambda a: jnp.concatenate(
                [a[2 * pair : 2 * pair + 1], a[2 * pair + 1 : 2 * pair + 2]], axis=1
            )
            onehot = jnp.where(sub_iota == two(lane), 1.0, 0.0).astype(BF16)
            pairs.append((onehot, jnp.broadcast_to(two(chunk), (8, 2 * SLOTS))))
        heads = []
        for pair, (onehot, chunk_of) in enumerate(pairs):
            dev = pick(pool, chunk_of, onehot)
            msg_out[step, 2 * pair] = dev[:, :SLOTS].astype(BF16)
            msg_out[step, 2 * pair + 1] = dev[:, SLOTS:].astype(BF16)
            rows = jnp.dot(mean_pool[...], onehot, preferred_element_type=F32)
            turned = chunk_of - row_iota
            found = jnp.zeros((8, 2 * SLOTS), F32)
            for k in range(CHUNKS // 8):
                found = jnp.where(turned == 8 * k, rows[8 * k : 8 * k + 8], found)
            found = jnp.sum(found, axis=0, keepdims=True)
            heads.extend([found[:, :SLOTS], found[:, SLOTS:]])
        msg_out[step, SHARE] = jnp.concatenate(heads, axis=0).astype(BF16)

        @pl.when(step < GROUP - 1)
        def _():
            pltpu.make_async_remote_copy(
                src_ref=msg_out.at[step],
                dst_ref=msg_in.at[me],
                send_sem=msg_send,
                recv_sem=msg_recv,
                device_id={"mem": to},
                device_id_type=MESH,
            ).start()

        @pl.when(step == GROUP - 1)
        def _():
            pltpu.make_async_copy(msg_out.at[step], msg_in.at[me], msg_own).start()
            for pair, (onehot, chunk_of) in enumerate(pairs):
                got = pick(val_pool, chunk_of, onehot)
                got = got[0:2] + got[2:4] + got[4:6]
                obs_own[2 * pair : 2 * pair + 1, :] = got[0:1, :SLOTS]
                obs_own[2 * pair + 1 : 2 * pair + 2, :] = got[0:1, SLOTS:]
                rate_own[2 * pair : 2 * pair + 1, :] = got[1:2, :SLOTS]
                rate_own[2 * pair + 1 : 2 * pair + 2, :] = got[1:2, SLOTS:]

        return carry

    lax.fori_loop(0, GROUP, gather, 0)

    for patch in range(EARLY, SHARE):
        send_state(patch)

    msg_all = pltpu.make_async_remote_copy(
        src_ref=msg_out.at[pl.ds(0, GROUP - 1)],
        dst_ref=msg_in.at[pl.ds(0, GROUP - 1)],
        send_sem=msg_send,
        recv_sem=msg_recv,
        device_id={"mem": lax.rem(me + 1, GROUP)},
        device_id_type=MESH,
    )
    msg_all.wait_recv()
    pltpu.make_async_copy(msg_out.at[GROUP - 1], msg_in.at[me], msg_own).wait()

    eye = jnp.where(
        lax.broadcasted_iota(jnp.int32, (ENS, ENS), 0)
        == lax.broadcasted_iota(jnp.int32, (ENS, ENS), 1),
        1.0,
        0.0,
    ).astype(F32)
    lane_iota = lax.broadcasted_iota(jnp.int32, (1, SLOTS), 1)
    counts_row = counts_v[...].reshape(1, PATCHES).astype(F32)
    for p in range(SHARE):
        dev = msg_in[:, p].astype(F32)
        head = msg_in[:, SHARE].astype(F32)[:, p : p + 1, :]
        chosen = (dev + head).reshape(ENS, SLOTS)
        mean_obs = jnp.mean(chosen, axis=0, keepdims=True)
        spread = chosen - mean_obs
        count = jnp.sum(
            jnp.where(lane_iota == me * SHARE + p, counts_row, 0.0), axis=1, keepdims=True
        )
        used = lane_iota.astype(F32) < count
        rate = jnp.where(used, rate_own[p : p + 1, :] * weights_v[p : p + 1, :], 0.0)
        misfit = obs_own[p : p + 1, :] - mean_obs
        system = mm_t(spread * rate, spread) + (ENS - 1.0) * eye
        square = jnp.sum(system * system, axis=1, keepdims=True)
        frob = jnp.sqrt(jnp.sum(square, axis=0, keepdims=True))
        pulled_s[p] = mm_t(jnp.broadcast_to(rate * misfit, (8, SLOTS)), spread)
        frob_s[p] = jnp.broadcast_to(frob, (8, SLOTS))
        scaled = system / frob
        change = 0.5 * (eye - scaled)
        root[p, :ENS] = eye + change
        root[p, ENS:] = scaled + mm(scaled, change)

    def sweep(step, carry):
        for p in range(SHARE):
            both = root[p]
            change = 0.5 * (eye - mm(both[:ENS], both[ENS:]))
            root[p] = both + mm(both, change)
        return carry

    lax.fori_loop(1, NS - 1, sweep, 0)
    for p in range(SHARE):
        both = root[p]
        inverse = both[:ENS]
        change = 0.5 * (eye - mm(inverse, both[ENS:]))
        inverse = inverse + mm(inverse, change)
        inv_half = inverse / jnp.sqrt(frob_s[p][0:1, :])
        shift = mm(mm(pulled_s[p], inv_half), inv_half)[0:1]
        trans[p] = (math.sqrt(ENS - 1.0) * inv_half + shift).astype(BF16)

    def analyse(p, carry):
        pltpu.make_async_remote_copy(
            src_ref=state.at[pl.ds(0, GROUP - 1)],
            dst_ref=state_in.at[p, pl.ds(0, GROUP - 1)],
            send_sem=state_send,
            recv_sem=state_recv.at[p],
            device_id={"mem": lax.rem(me + 1, GROUP)},
            device_id_type=MESH,
        ).wait_recv()
        own_state(p).wait()

        def widen(source, carry):
            for m in range(SHARE):
                block = state_in[p, source, m].astype(F32)
                for half in range(2):
                    wide[half, pl.ds(source * SHARE + m, 4, stride=ENS), :] = block[
                        :, 128 * half : 128 * half + 128
                    ]
            return carry

        lax.fori_loop(0, GROUP, widen, 0)
        mix = trans[p]
        for level in range(4):
            for half in range(2):
                rows = slice(ENS * level, ENS * level + ENS)
                block = wide[half, rows, :]
                mean_state = jnp.mean(block, axis=0, keepdims=True)
                perturb = (block - mean_state).astype(BF16)
                mixed[half, rows, :] = (
                    jnp.dot(mix, perturb, preferred_element_type=F32) + mean_state
                )

        def narrow(step, carry):
            to = lax.rem(me + 5 * step, GROUP)
            for m in range(SHARE):
                block = jnp.concatenate(
                    [
                        mixed[half, pl.ds(to * SHARE + m, 4, stride=ENS), :]
                        for half in range(2)
                    ],
                    axis=1,
                )
                back[p, to, m] = block.astype(BF16)

            @pl.when((step > 0) & (p < HOLD))
            def _():
                pltpu.make_async_remote_copy(
                    src_ref=back.at[p, to],
                    dst_ref=out.at[me * SHARE + p],
                    send_sem=back_send,
                    recv_sem=back_recv,
                    device_id={"mem": to},
                    device_id_type=MESH,
                ).start()

            @pl.when(step == 0)
            def _():
                pltpu.make_async_copy(
                    back.at[p, me], out.at[me * SHARE + p], back_own.at[p]
                ).start()

            return carry

        lax.fori_loop(0, GROUP, narrow, 0)
        return carry

    lax.fori_loop(0, SHARE, analyse, 0)

    def rest(turn, carry):
        mine = me // 2
        chip = jnp.where(turn < 4, turn, 4 + lax.rem(mine + turn, 4))

        def one(k, carry):
            p = HOLD + k // 2
            to = chip * 2 + 1 - lax.rem(k, 2)

            @pl.when(to != me)
            def _():
                pltpu.make_async_remote_copy(
                    src_ref=back.at[p, to],
                    dst_ref=out.at[me * SHARE + p],
                    send_sem=back_send,
                    recv_sem=back_recv,
                    device_id={"mem": to},
                    device_id_type=MESH,
                ).start()

            return carry

        lax.fori_loop(0, 2 * (SHARE - HOLD), one, 0)
        return carry

    lax.fori_loop(0, GROUP // 2, rest, 0)

    others = (GROUP - 1) * SHARE
    msg_all.wait_send()
    for ref, send in ((state, state_send), (out, back_send)):
        whole = pltpu.make_async_remote_copy(
            src_ref=ref.at[pl.ds(0, others)],
            dst_ref=out.at[pl.ds(0, others)],
            send_sem=send,
            recv_sem=back_recv,
            device_id={"mem": lax.rem(me + 1, GROUP)},
            device_id_type=MESH,
        )
        whole.wait_send()
    whole.wait_recv()
    for p in range(SHARE):
        pltpu.make_async_copy(back.at[p, me], out.at[me * SHARE + p], back_own.at[p]).wait()


def body(state, obs_ens, obs_values, obs_index, patch_count, slot_weight):
    vmem, dma = pltpu.VMEM, pltpu.SemaphoreType.DMA
    block = state.shape[1:]
    scratch = [
        vmem(obs_ens.shape, F32),
        vmem(obs_values.shape, F32),
        vmem((8,) + obs_ens.shape[:3] + (RIM,), F32),
        vmem((8,) + obs_values.shape[:3] + (RIM,), F32),
        vmem(obs_index.shape, jnp.int32),
        vmem((SHARE, SLOTS), F32),
        vmem(patch_count.shape, jnp.int32),
        vmem((CHUNKS * 8, CHUNK), BF16),
        vmem((CHUNKS, CHUNK), F32),
        vmem((CHUNKS, CHUNK), BF16),
        vmem((CHUNKS * 8, CHUNK), BF16),
        vmem((SHARE, SLOTS), F32),
        vmem((SHARE, SLOTS), F32),
        vmem((GROUP, MSG, SHARE, SLOTS), BF16),
        vmem((GROUP, MSG, SHARE, SLOTS), BF16),
        vmem((SHARE, GROUP) + block, BF16),
        vmem((SHARE, 2 * ENS, ENS), F32),
        vmem((SHARE, 8, SLOTS), F32),
        vmem((SHARE, 8, SLOTS), F32),
        vmem((SHARE, ENS, ENS), BF16),
        vmem((2, 4 * ENS, 128), F32),
        vmem((2, 4 * ENS, 128), F32),
        vmem((SHARE, GROUP) + block, BF16),
        dma((5,)),
        dma((8,)), dma((8,)), dma((8,)), dma((8,)),
        dma, dma, dma,
        dma, dma((SHARE,)), dma((SHARE,)),
        dma, dma, dma((SHARE,)),
        pltpu.SemaphoreType.REGULAR, pltpu.SemaphoreType.REGULAR,
    ]
    return pl.pallas_call(
        kernel,
        out_shape=pltpu.VMEM(state.shape, state.dtype),
        in_specs=[pl.BlockSpec(memory_space=pl.ANY)] * 6,
        out_specs=pl.BlockSpec(memory_space=pltpu.VMEM),
        scratch_shapes=scratch,
        compiler_params=pltpu.CompilerParams(
            collective_id=0, has_side_effects=True, vmem_limit_bytes=40 * 2**20
        ),
        name="letkf",
    )(*[
        pltpu.with_memory_space_constraint(a, pltpu.HBM)
        for a in (state, obs_ens, obs_values, obs_index, patch_count, slot_weight)
    ])


def solution(mesh):
    placed = (
        P(("gx", "gy"), "mem", None, None),
        P("mem", "gx", "gy", None),
        P(None, "gx", "gy", None),
        P(("gx", "gy"), None),
        P(("gx", "gy")),
        P(("gx", "gy"), None),
    )
    return jax.shard_map(
        body,
        mesh=mesh,
        in_specs=placed,
        out_specs=P(("gx", "gy"), "mem", None, None),
        check_vma=False,
    )
```
